32 devices in a mesh: dp: 4 (over z), row: 2 (over x), col: 4 (over y, core).
Axes of the slice: x: 2, y: 2, z: 4, core: 2. Of those that a mesh axis runs over, the one named last changes fastest.
Arguments:
- residual_in: bfloat16 [8192, 2048], P(('dp', 'col'), 'row'), may hold values from -6 to 6
- attn_gain: float32 [2048], P('row'), may hold values from 0.5 to 1.5
- attn_shift: float32 [2048], P('row'), may hold values from -1.75 to 1.75
- mlp_gain: float32 [2048], P('row'), may hold values from 0.5 to 1.5
- mlp_shift: float32 [2048], P('row'), may hold values from -1.75 to 1.75
- qkv_weight: bfloat16 [2048, 8, 768], P('row', 'col'), may hold values from -0.125 to 0.125
- qkv_bias: float32 [8, 768], P('col'), may hold values from -1.75 to 1.75
- dense_weight: bfloat16 [8, 256, 2048], P('col', None, 'row'), may hold values from -1 to 1
- dense_bias: float32 [2048], P('row'), may hold values from -1.75 to 1.75
- in_weight: bfloat16 [2048, 8192], P('row', 'col'), may hold values from -1 to 1
- in_bias: float32 [8192], P('col'), may hold values from -1.75 to 1.75
- out_weight: bfloat16 [8192, 2048], P('col', 'row'), may hold values from -0.0625 to 0.0625
- out_bias: float32 [2048], P('row'), may hold values from -1.75 to 1.75
- cotangent: bfloat16 [8192, 2048], P(('dp', 'col'), 'row'), may hold values from -6 to 6
Outputs:
- block_out: bfloat16 [8192, 2048], P(('dp', 'col'), 'row')
- input_grad: float32 [8192, 2048], P(('dp', 'col'), 'row')
- attn_gain_grad: float32 [2048], P('row')
- attn_shift_grad: float32 [2048], P('row')
- mlp_gain_grad: float32 [2048], P('row')
- mlp_shift_grad: float32 [2048], P('row')
- qkv_weight_grad: float32 [2048, 8, 768], P('row', 'col')
- qkv_bias_grad: float32 [8, 768], P('col')
- dense_weight_grad: float32 [8, 256, 2048], P('col', None, 'row')
- dense_bias_grad: float32 [2048], P('row')
- in_weight_grad: float32 [2048, 8192], P('row', 'col')
- in_bias_grad: float32 [8192], P('col')
- out_weight_grad: float32 [8192, 2048], P('col', 'row')
- out_bias_grad: float32 [2048], P('row')
The draws below stay inside these ranges and needn't reach their ends.
All inputs are finite; a program needn't handle non-finite values.
Results may differ from the reference program's by a relative error of at most 0.011.
Values may be sent and summed in bfloat16 or wider, within the bound.
No kernel may reach another device: no remote copies, remote signals or barrier semaphores. Data moves between devices by JAX's collectives and lax.ppermute only.
A program may use at most 256 MiB of HBM per device.

```python
import jax
import jax.numpy as jnp
from jax import lax

D = 2048
HEADS = 8
HS = 256
FF = 8192
ROT = 64
LENGTH = 2048
SEQS = 4
TOKENS = 8192


def draw_in_weight(key, part):
    key = jax.random.fold_in(key, 11)
    entry_key, column_key = jax.random.split(key)
    entries = jnp.clip(jax.random.normal(entry_key, (D, FF), jnp.float32), -4.0, 4.0)
    columns = 0.5 * jnp.clip(jax.random.normal(column_key, (FF,), jnp.float32), -3.0, 3.0)
    return ((entries + columns[None, :]) * D ** (-0.5)).astype(jnp.bfloat16)


def shard_levels(rng, shape, shards, low, top_value):
    factor_of, own = 1.0, jax.random.fold_in(rng, 6)
    for axis_at, parts in shards:
        draws = jnp.exp(jax.random.uniform(jax.random.fold_in(own, axis_at), (parts,), jnp.float32, low / len(shards), top_value / len(shards)))
        factor_of = factor_of * jnp.repeat(draws, shape[axis_at] // parts).reshape([-1 if axis == axis_at else 1 for axis in range(len(shape))])
    return factor_of


def scatter_about(own_key, extent, width, bound, cuts=(), held_as=jnp.bfloat16):
    array = jax.random.normal(own_key, extent, jnp.float32) * width
    if len(cuts) > 0:
        array = shard_levels(own_key, extent, cuts, -0.22, 0.18) * array
    return jnp.clip(array, min=-bound, max=bound).astype(held_as)


def setup_inputs(seed: int = 0) -> dict:
    keys = jax.random.split(jax.random.key(seed), 15)
    return {
        "residual_in": scatter_about(keys[0], (TOKENS, D), 1.0, 6.0, ((0, 16), (1, 2))),
        "attn_gain": jnp.clip(1.0 + 0.1 * jax.random.normal(keys[1], (D,), jnp.float32), 0.5, 1.5),
        "attn_shift": scatter_about(keys[2], (D,), 0.3, 1.75, ((0, 2),), jnp.float32),
        "mlp_gain": jnp.clip(1.0 + 0.1 * jax.random.normal(keys[3], (D,), jnp.float32), 0.5, 1.5),
        "mlp_shift": scatter_about(keys[4], (D,), 0.3, 1.75, ((0, 2),), jnp.float32),
        "qkv_weight": scatter_about(keys[5], (D, HEADS, 3 * HS), D ** -0.5, 0.125, ((0, 2), (1, 4))),
        "qkv_bias": scatter_about(keys[6], (HEADS, 3 * HS), 0.3, 1.75, ((0, 4),), jnp.float32),
        "dense_weight": scatter_about(keys[7], (HEADS, HS, D), (max(HEADS * HS // 64, 4)) ** -0.5, 1.0, ((0, 4), (2, 2))),
        "dense_bias": scatter_about(keys[8], (D,), 0.3, 1.75, ((0, 2),), jnp.float32),
        "in_weight": draw_in_weight(jax.random.fold_in(keys[14], 71), 0),
        "in_bias": scatter_about(keys[10], (FF,), 0.3, 1.75, ((0, 4),), jnp.float32),
        "out_weight": scatter_about(keys[11], (FF, D), FF ** -0.5, 0.0625, ((0, 4), (1, 2))),
        "out_bias": scatter_about(keys[12], (D,), 0.3, 1.75, ((0, 2),), jnp.float32),
        "cotangent": scatter_about(keys[13], (TOKENS, D), 1.0, 6.0, ((0, 16), (1, 2))),
    }


EPSILON = 1e-05
ROPE_BASE = 10000.0
NEGATIVE = -1e+30
HIGHEST = lax.Precision.HIGHEST

@jax.custom_vjp
def low(v):
    return lax.optimization_barrier(v.astype(jnp.bfloat16)).astype(jnp.float32)

@jax.custom_vjp
def low_back(v):
    return v

def low_keep(v):
    return (low(v), None)

def low_pass(kept, grad):
    return (grad,)

def back_keep(v):
    return (v, None)

def back_low(kept, grad):
    return (low(grad),)
low.defvjp(low_keep, low_pass)
low_back.defvjp(back_keep, back_low)

def rotary_tables():
    half_rot = ROT // 2
    position = jnp.arange(LENGTH).astype(jnp.float32)
    frequency = ROPE_BASE ** (-(2.0 * jnp.arange(half_rot).astype(jnp.float32)) / ROT)
    angles = position[:, None] * frequency[None, :]
    return (jnp.cos(angles)[:, None, :], jnp.sin(angles)[:, None, :])

def rotate(values, cos_table, sin_table):
    half_rot = ROT // 2
    lower_half = values[..., :half_rot]
    upper_half = values[..., half_rot:ROT]
    return jnp.concatenate([lower_half * cos_table - upper_half * sin_table, upper_half * cos_table + lower_half * sin_table, values[..., ROT:]], -1)

def attend_one(pieces):
    query_rows, key_rows, value_rows = pieces
    raw_scores = jnp.einsum('qhe,khe->hqk', query_rows, key_rows, precision=HIGHEST) * HS ** (-0.5)
    scores = low_back(raw_scores)
    places = jnp.arange(LENGTH)
    causal_mask = places[None, :] <= places[:, None]
    scores = jnp.where(causal_mask[None], scores, NEGATIVE)
    row_max = lax.optimization_barrier(jnp.max(scores, -1, keepdims=True))
    exp_scores = jnp.exp(scores - row_max)
    prob_rows = low(exp_scores / lax.optimization_barrier(jnp.sum(exp_scores, -1, keepdims=True)))
    return jnp.einsum('hqk,khe->qhe', prob_rows, value_rows, precision=HIGHEST)

def forward(residual_in, attn_gain, attn_shift, mlp_gain, mlp_shift, qkv_weight, qkv_bias, dense_weight, dense_bias, in_weight, in_bias, out_weight, out_bias):
    average = lax.optimization_barrier(jnp.mean(residual_in, -1, keepdims=True))
    squares = lax.optimization_barrier(jnp.mean(residual_in * residual_in, -1, keepdims=True))
    normed = (residual_in - average) * lax.rsqrt(squares - average * average + EPSILON)
    attn_input = low(normed * attn_gain + attn_shift)
    mlp_input = low(normed * mlp_gain + mlp_shift)
    packed = low_back(jnp.einsum('td,dhe->the', attn_input, qkv_weight, precision=HIGHEST) + qkv_bias)
    cos_table, sin_table = rotary_tables()
    shaped = packed.reshape(SEQS, LENGTH, HEADS, 3 * HS)
    query_rows = low(rotate(shaped[..., :HS], cos_table, sin_table))
    key_rows = low(rotate(shaped[..., HS:2 * HS], cos_table, sin_table))
    value_rows = low(shaped[..., 2 * HS:])
    attended = lax.map(jax.checkpoint(attend_one), (query_rows, key_rows, value_rows))
    attended = low_back(low(attended.reshape(TOKENS, HEADS, HS)))
    pre_act = low_back(jnp.dot(mlp_input, in_weight, precision=HIGHEST) + in_bias)
    active = low(jax.nn.gelu(pre_act, approximate=False))
    attn_branch = jnp.einsum('the,hed->td', attended, dense_weight, precision=HIGHEST) + dense_bias
    mlp_branch = jnp.dot(active, out_weight, precision=HIGHEST) + out_bias
    return residual_in + attn_branch + mlp_branch

def reference(residual_in, attn_gain, attn_shift, mlp_gain, mlp_shift, qkv_weight, qkv_bias, dense_weight, dense_bias, in_weight, in_bias, out_weight, out_bias, cotangent):
    params = (residual_in, attn_gain, attn_shift, mlp_gain, mlp_shift, qkv_weight, qkv_bias, dense_weight, dense_bias, in_weight, in_bias, out_weight, out_bias)
    params = tuple((item.astype(jnp.float32) for item in params))
    result, pullback = jax.vjp(forward, *params)
    grads = pullback(cotangent.astype(jnp.float32))
    return (result.astype(jnp.bfloat16), grads[0], grads[1], grads[2], grads[3], grads[4], grads[5], grads[6], grads[7], grads[8], grads[9], grads[10], grads[11], grads[12])
```

```python
import math

import jax
import jax.numpy as jnp
from jax import lax
from jax.experimental import pallas as pl
from jax.experimental.pallas import tpu as pltpu
from jax.sharding import PartitionSpec as P

HS = 256
ROT = 64
LENGTH = 2048
LANES = 128
EPSILON = 1e-05
ROPE_BASE = 10000.0
NEGATIVE = -1e30
BF = jnp.bfloat16
F32 = jnp.float32
NN, NT, TN = ((1,), (0,)), ((1,), (1,)), ((0,), (0,))
MIB = 2**20
COST = pl.CostEstimate(flops=0, bytes_accessed=0, transcendentals=0)


def tie(value, *others):
    return lax.optimization_barrier((value,) + others)[0]


def swap_row(value):
    return lax.ppermute(value, "row", [(0, 1), (1, 0)])


def swap_col(value, bit):
    return lax.ppermute(value, "col", [(i, i ^ bit) for i in range(lax.axis_size("col"))])


def swap_y(value):
    return swap_col(value, 2)


def swap_core(value):
    return swap_col(value, 1)


def half(array, axis, index):
    size = array.shape[axis] // 2
    return lax.dynamic_slice_in_dim(array, index * size, size, axis)


def dot(a, b, dims):
    return lax.dot_general(a, b, (dims, ((), ())), preferred_element_type=F32)


def rotary_tables(tokens):
    position = (jnp.arange(tokens) % LENGTH).astype(F32)
    lane = jnp.arange(LANES)
    index = (lane % (ROT // 2)).astype(F32)
    frequency = ROPE_BASE ** (-(2.0 * index) / ROT)
    angle = position[:, None] * frequency[None, :]
    cos = jnp.where(lane < ROT, jnp.cos(angle), 1.0)
    sin = jnp.sin(angle)
    low = jnp.where(lane < ROT // 2, -sin, 0.0)
    high = jnp.where((lane >= ROT // 2) & (lane < ROT), sin, 0.0)
    return cos, low, high


def rotate(values, cos, low, high):
    first = values[:, :LANES]
    up = pltpu.roll(first, LANES - ROT // 2, 1)
    down = pltpu.roll(first, ROT // 2, 1)
    first = first * cos + up * low + down * high
    return jnp.concatenate([first, values[:, LANES:]], 1)


def tiled(i, *_):
    return (i, 0)


def fixed(*_):
    return (0, 0)


def call(kernel, name, steps, ins, outs, col=None, vmem=40, tile=None):
    def block(shape, index, rows=None):
        rows = rows or (shape[0] if index is fixed else tile or shape[0] // steps)
        return pl.BlockSpec((rows, shape[1]), index)

    spec = pltpu.PrefetchScalarGridSpec(
        num_scalar_prefetch=0 if col is None else 1,
        grid=(steps,),
        in_specs=[block(a.shape, index) for a, index in ins],
        out_specs=tuple(block(shape, index, rows) for shape, _, rows, index in outs),
    )
    return pl.pallas_call(
        kernel if col is None else lambda _, *refs: kernel(*refs),
        grid_spec=spec,
        out_shape=tuple(jax.ShapeDtypeStruct(shape, dtype) for shape, dtype, _, _ in outs),
        compiler_params=pltpu.CompilerParams(vmem_limit_bytes=vmem * MIB),
        cost_estimate=COST,
        name=name,
    )(*([] if col is None else [col.reshape(1)]), *[a for a, _ in ins])


def normed_halves(x_ref, y_ref):
    x, y = x_ref[...].astype(F32), y_ref[...].astype(F32)
    width = x.shape[1] + y.shape[1]
    average = (jnp.sum(x, 1, keepdims=True) + jnp.sum(y, 1, keepdims=True)) / width
    squares = (jnp.sum(x * x, 1, keepdims=True) + jnp.sum(y * y, 1, keepdims=True)) / width
    scale = lax.rsqrt(squares - average * average + EPSILON)
    return (x - average) * scale, (y - average) * scale


def norm_kernel(x_ref, y_ref, gx_ref, gy_ref, ax_ref, ay_ref, mx_ref, my_ref):
    x, y = normed_halves(x_ref, y_ref)
    ax_ref[...] = (x * gx_ref[0:1] + gx_ref[1:2]).astype(BF)
    ay_ref[...] = (y * gy_ref[0:1] + gy_ref[1:2]).astype(BF)
    mx_ref[...] = (x * gx_ref[2:3] + gx_ref[3:4]).astype(BF)
    my_ref[...] = (y * gy_ref[2:3] + gy_ref[3:4]).astype(BF)


def norm_call(col, flip, x, y, gx, gy, *before):
    (rows, feats), tile, slots = x.shape, 256, 4
    steps = rows // tile

    def index(i, col_ref):
        return ((col_ref[0] ^ flip) * steps + i, 0)

    rest = [pl.BlockSpec(memory_space=pl.ANY)] * len(before)
    block = pl.BlockSpec((tile, feats), tiled)
    whole = pl.BlockSpec(gx.shape, fixed)
    return pl.pallas_call(
        lambda _, x, y, gx, gy, *refs: norm_kernel(x, y, gx, gy, *refs[len(before) :]),
        grid_spec=pltpu.PrefetchScalarGridSpec(
            num_scalar_prefetch=1,
            grid=(steps,),
            in_specs=[block, block, whole, whole] + rest,
            out_specs=(pl.BlockSpec((tile, feats), index),) * 4,
        ),
        out_shape=(jax.ShapeDtypeStruct((slots * rows, feats), BF),) * 4,
        input_output_aliases={5 + i: i for i in range(len(before))},
        compiler_params=pltpu.CompilerParams(vmem_limit_bytes=56 * MIB),
        cost_estimate=COST,
        name="norm",
    )(col.reshape(1), x, y, gx, gy, *before)


def pre_kernel(x_ref, y_ref, wx_ref, wy0_ref, wy1_ref, bias_ref, active_ref, slope_ref):
    mid, part = wy0_ref.shape[0], wx_ref.shape[1]
    for start in range(0, wx_ref.shape[1], part):
        at = slice(start, start + part)
        u = dot(x_ref[...], wx_ref[:, at], NN) + bias_ref[:, at]
        u = u + dot(y_ref[:, :mid], wy0_ref[:, at], NN) + dot(y_ref[:, mid:], wy1_ref[:, at], NN)
        phi = 0.5 * (1.0 + lax.erf(u * 2.0**-0.5))
        bell = jnp.exp(-0.5 * u * u)
        active_ref[:, at] = (u * phi).astype(BF)
        slope_ref[:, at] = (phi + u * bell * (2.0 * math.pi) ** (-0.5)).astype(BF)


def pre_call(x, y, wx, wy0, wy1, bias):
    tokens, tile, units = x.shape[0], 256, wx.shape[1]
    return call(
        pre_kernel,
        "pre_act",
        tokens // tile,
        [(x, tiled), (y, tiled), (wx, fixed), (wy0, fixed), (wy1, fixed), (bias.reshape(1, -1), fixed)],
        [((tokens, units), BF, tile, tiled)] * 2,
        vmem=56,
    )


def rowwise(fn, rows, outs, *ins, flag=None):
    tile = 256
    ins = [i if isinstance(i, tuple) else (i, 0) for i in ins]
    flags = [] if flag is None else [flag.astype(jnp.int32).reshape(1)]

    def at(first):
        return fixed if first is None else lambda i, *_: (i + first // tile, 0)

    def kernel(*refs):
        values = [ref[0] != 0 for ref in refs[: len(flags)]]
        refs = refs[len(flags) :]
        results = fn(*values, *[ref[...] for ref in refs[: len(ins)]])
        for ref, result in zip(refs[len(ins) :], results, strict=True):
            ref[...] = result

    return pl.pallas_call(
        kernel,
        grid_spec=pltpu.PrefetchScalarGridSpec(
            num_scalar_prefetch=len(flags),
            grid=(rows // tile,),
            in_specs=[pl.BlockSpec((tile, a.shape[1]), at(first)) for a, first in ins],
            out_specs=tuple(pl.BlockSpec((tile, cols), tiled) for cols, _ in outs),
        ),
        out_shape=tuple(jax.ShapeDtypeStruct((rows, cols), dtype) for cols, dtype in outs),
        compiler_params=pltpu.CompilerParams(vmem_limit_bytes=32 * MIB),
        cost_estimate=COST,
        name="rowwise",
    )(*flags, *[a for a, _ in ins])


def plain_add(a, b):
    return [(a.astype(F32) + b.astype(F32)).astype(BF)]


def add_low(a, b):
    return (a.astype(F32) + b.astype(F32)).astype(a.dtype)


def choose(flag):
    def fn(held, arrived):
        if held.ndim == 1:
            return jnp.where(flag, arrived, held)
        outs = [(held.shape[1], BF)]
        return rowwise(lambda f, h, a: [jnp.where(f, a, h)], held.shape[0], outs, held, arrived, flag=flag)[0]

    return fn


def choose_or_add(flag):
    return lambda value, a, b: jnp.where(flag, value, add_low(a, b))


def weight_grad(cuts, a, b, last_a=None, last_b=None):
    tokens, cols, tile = b.shape[0], b.shape[1], 256
    own = sum(cuts) // tile if last_a is None else a.shape[1] // tile
    skip = 0
    if isinstance(a, tuple):
        a, skip = a[0], a[1] // tile
    first = [sum(cuts[:i]) // tile for i in range(len(cuts) + 1)]

    def kernel(*refs):
        step = pl.program_id(0)

        def store(out):
            for start, end, ref in zip(first[:-1], first[1:], refs[-len(cuts) :], strict=True):

                @pl.when((step >= start) & (step < end))
                def _():
                    ref[...] = out

        if last_a is None:
            store(dot(refs[0][...], refs[1][...], TN).astype(BF))
            return

        @pl.when(step < own)
        def _():
            store(dot(refs[0][...], refs[1][...], TN).astype(BF))

        @pl.when(step >= own)
        def _():
            store(dot(refs[2][...], refs[3][...], TN).astype(BF))

    def index(start, end):
        return lambda i: (jnp.clip(i - start, 0, end - start - 1), 0)

    ins = [a, b] if last_a is None else [a, b, last_a, last_b]
    specs = [
        pl.BlockSpec((tokens, tile), lambda i: (0, jnp.minimum(i, own - 1) + skip)),
        pl.BlockSpec(b.shape, fixed),
        pl.BlockSpec((tokens, tile), fixed),
        pl.BlockSpec(b.shape, fixed),
    ]
    return pl.pallas_call(
        kernel,
        grid=(first[-1],),
        out_shape=tuple(jax.ShapeDtypeStruct((size, cols), BF) for size in cuts),
        in_specs=specs[: len(ins)],
        out_specs=tuple(
            pl.BlockSpec((tile, cols), index(s, e)) for s, e in zip(first[:-1], first[1:], strict=True)
        ),
        compiler_params=pltpu.CompilerParams(vmem_limit_bytes=40 * MIB),
        cost_estimate=COST,
        name="weight_grad",
    )(*ins)


def pre_grad_kernel(gx_ref, gy_ref, wx_ref, wy0_ref, wy1_ref, slope_ref, out_ref, sum_ref):
    @pl.when(pl.program_id(0) == 0)
    def _():
        sum_ref[...] = jnp.zeros_like(sum_ref)

    mid = wy0_ref.shape[0]
    for i, wy_ref in enumerate((wy0_ref, wy1_ref)):
        at = slice(i * mid, (i + 1) * mid)
        u = dot(gx_ref[...], wx_ref[at, :], NT) + dot(gy_ref[...], wy_ref[...], NT)
        low = (u * slope_ref[:, at].astype(F32)).astype(BF)
        out_ref[:, at] = low
        sum_ref[:, at] += jnp.sum(low.astype(F32), 0, keepdims=True)


def pre_grad_call(gx, gy, wx, wy0, wy1, slope):
    tokens, tile, units = gx.shape[0], 512, wx.shape[0]
    return call(
        pre_grad_kernel,
        "pre_grad",
        tokens // tile,
        [(gx, tiled), (gy, tiled), (wx, fixed), (wy0, fixed), (wy1, fixed), (slope, tiled)],
        [((tokens, units), BF, tile, tiled), ((1, units), F32, 1, fixed)],
    )


def packed_kernel(x_ref, y_ref, wx_ref, wy_ref, bias_ref, cos_ref, low_ref, high_ref, q_ref, k_ref, v_ref):
    out = dot(x_ref[...], wx_ref[...], NN) + dot(y_ref[...], wy_ref[...], NN) + bias_ref[...]
    tables = cos_ref[...], low_ref[...], high_ref[...]
    q_ref[...] = rotate(out[:, :HS], *tables).astype(BF)
    k_ref[...] = rotate(out[:, HS : 2 * HS], *tables).astype(BF)
    v_ref[...] = out[:, 2 * HS :].astype(BF)


def packed_call(x, y, wx, wy, bias, *tables):
    tokens, tile = x.shape[0], 512
    return call(
        packed_kernel,
        "packed",
        tokens // tile,
        [(x, tiled), (y, tiled), (wx, fixed), (wy, fixed), (bias.reshape(1, -1), fixed)]
        + [(t, tiled) for t in tables],
        [((tokens, HS), BF, tile, tiled)] * 3,
    )


def attention_kernel(
    q_ref, k_ref, v_ref, g_ref, cos_ref, low_ref, high_ref, o_ref, out_ref, sum_ref, dk_acc, dv_acc
):
    slots, rows, _ = q_ref.shape
    scale = HS ** (-0.5)
    mask = lax.broadcasted_iota(jnp.int32, (rows, rows), 1) <= lax.broadcasted_iota(
        jnp.int32, (rows, rows), 0
    )
    total_sum = [jnp.zeros((1, HS), F32) for _ in range(3)]

    def unrotate(values, at):
        return rotate(values, cos_ref[at], -low_ref[at], -high_ref[at]).astype(BF)

    for i in range(slots):
        q, g = q_ref[i], g_ref[i]
        scores = []
        for j in range(i + 1):
            s = dot(q, k_ref[j], NT) * scale
            scores.append(jnp.where(mask, s, NEGATIVE) if j == i else s)
        top = scores[0].max(-1, keepdims=True)
        for s in scores[1:]:
            top = jnp.maximum(top, s.max(-1, keepdims=True))
        exps = [jnp.exp(s - top) for s in scores]
        inv = 1.0 / sum(e.sum(-1, keepdims=True) for e in exps)
        probs = [e * inv for e in exps]
        out = jnp.zeros((rows, HS), F32)
        center = jnp.zeros((rows, 1), F32)
        prob_grads = []
        for j in range(i + 1):
            low = probs[j].astype(BF)
            v = v_ref[j]
            out = out + dot(low, v, NN)
            pg = dot(g, v, NT)
            center = center + (probs[j] * pg).sum(-1, keepdims=True)
            prob_grads.append(pg)
            dv = dot(low, g, TN)
            if j == i:
                dv_acc[j] = dv
            else:
                dv_acc[j] += dv
        o_ref[i] = out.astype(BF)
        dq = jnp.zeros((rows, HS), F32)
        for j in range(i + 1):
            sg = (probs[j] * (prob_grads[j] - center)).astype(BF)
            dq = dq + dot(sg, k_ref[j], NN)
            dk = dot(sg, q, TN)
            if j == i:
                dk_acc[j] = dk
            else:
                dk_acc[j] += dk
        dq = unrotate(dq * scale, i)
        out_ref[i, :, 0:HS] = dq
        total_sum[0] = total_sum[0] + jnp.sum(dq.astype(F32), 0, keepdims=True)
    for j in range(slots):
        dk = unrotate(dk_acc[j] * scale, j)
        dv = dv_acc[j].astype(BF)
        out_ref[j, :, HS : 2 * HS] = dk
        out_ref[j, :, 2 * HS :] = dv
        total_sum[1] = total_sum[1] + jnp.sum(dk.astype(F32), 0, keepdims=True)
        total_sum[2] = total_sum[2] + jnp.sum(dv.astype(F32), 0, keepdims=True)
    for i in range(3):
        sum_ref[:, i * HS : (i + 1) * HS] = total_sum[i]


def attention(slots, q, k, v, g, cos, low, high):
    tokens = q.shape[0]
    rows = tokens // slots
    vmem = pl.BlockSpec(memory_space=pltpu.VMEM)
    attended, packed_grad, sums = pl.pallas_call(
        attention_kernel,
        out_shape=(
            jax.ShapeDtypeStruct((slots, rows, HS), BF),
            jax.ShapeDtypeStruct((slots, rows, 3 * HS), BF),
            jax.ShapeDtypeStruct((1, 3 * HS), F32),
        ),
        in_specs=[vmem] * 7,
        out_specs=(vmem,) * 3,
        scratch_shapes=[pltpu.VMEM((slots, rows, HS), F32)] * 2,
        compiler_params=pltpu.CompilerParams(vmem_limit_bytes=56 * MIB),
        cost_estimate=COST,
        name="attention",
    )(*[a.reshape(slots, rows, a.shape[1]) for a in (q, k, v, g, cos, low, high)])
    return packed_grad.reshape(tokens, 3 * HS), attended.reshape(tokens, HS), sums


def mixed_kernel(a_ref, b_ref, dx_ref, dy_ref, wx_ref, wy0_ref, wy1_ref, out_ref):
    feats, mid = dx_ref.shape[1], wy0_ref.shape[0]
    a, b = a_ref[...], b_ref[...]
    out_ref[:, :feats] = (dot(a, dx_ref[...], NN) + dot(b, wx_ref[...], NN)).astype(BF)
    y = dot(a, dy_ref[...], NN) + dot(b[:, :mid], wy0_ref[...], NN) + dot(b[:, mid:], wy1_ref[...], NN)
    out_ref[:, feats:] = y.astype(BF)


def mixed_call(col, part, attended, active, dx, dy, *weights):
    tokens, tile, width = attended.shape[0] // 2, 256, dx.shape[1] + dy.shape[1]
    steps = tokens // tile
    each = steps // 2

    def order(i, col_ref):
        return ((col_ref[0] ^ part ^ (2 * (i // each))) * each + i % each, 0)

    ins = [(attended, order), (active, order)] + [(w, fixed) for w in (dx, dy, *weights)]
    outs = [((tokens, width), BF, tile, tiled)]
    return call(mixed_kernel, "mixed", steps, ins, outs, col, tile=tile)[0]


def norm_grad_kernel(
    x_ref, y_ref, gx_ref, gy_ref, p_ref, u_ref, qx_ref, qy_ref, wx_ref, wy0_ref, wy1_ref, out_ref, sum_ref
):
    feats, mid = x_ref.shape[1], wy0_ref.shape[0]

    @pl.when(pl.program_id(0) == 0)
    def _():
        sum_ref[...] = jnp.zeros_like(sum_ref)

    normed = normed_halves(x_ref, y_ref)
    p, u = p_ref[...], u_ref[...]
    for start in range(0, 2 * feats, mid):
        side, lo = divmod(start, feats)
        at, part = slice(start, start + mid), slice(lo, lo + mid)
        q = (qx_ref, qy_ref)[side][part, :]
        w = wx_ref[part, :] if side == 0 else (wy0_ref, wy1_ref)[lo // mid][...]
        gains = (gx_ref, gy_ref)[side][:, part]
        n = normed[side][:, part]
        a, m = dot(p, q, NT), dot(u, w, NT)
        out_ref[:, at] = (a * gains[0:1] + m * gains[2:3]).astype(BF)
        sum_ref[0:1, at] += jnp.sum(a * n, 0, keepdims=True)
        sum_ref[1:2, at] += jnp.sum(a, 0, keepdims=True)
        sum_ref[2:3, at] += jnp.sum(m * n, 0, keepdims=True)
        sum_ref[3:4, at] += jnp.sum(m, 0, keepdims=True)


def norm_grad_call(col, part, x, y, gx, gy, packed_grad, pre_grad, *weights):
    tokens, tile, width = x.shape[0], 256, x.shape[1] + y.shape[1]
    steps = tokens // tile
    each = steps // 2

    def order(i, col_ref):
        return ((col_ref[0] ^ part ^ (2 * (i // each))) * each + i % each, 0)

    ins = [(x, tiled), (y, tiled), (gx, fixed), (gy, fixed), (packed_grad, order), (pre_grad, order)]
    return call(
        norm_grad_kernel,
        "norm_grad",
        steps,
        ins + [(w, fixed) for w in weights],
        [((tokens, width), BF, tile, tiled), ((4, width), F32, 4, fixed)],
        col,
        tile=tile,
    )


def assemble(name, meta, arrays, steps, out, fill):
    flat = [a for _, _, part in arrays for a in part]
    shape, block, index = out

    def kernel(meta_ref, *refs):
        at = iter(refs[:-1])
        parts = [[next(at) for _ in part] for _, _, part in arrays]

        def read(i):
            values = [ref[...] for ref in parts[i]]
            value = values[0] if len(values) == 1 else jnp.where(meta_ref[1] != 0, *values)
            return value.astype(F32)

        fill(read, meta_ref[0], refs[-1])

    return pl.pallas_call(
        kernel,
        grid_spec=pltpu.PrefetchScalarGridSpec(
            num_scalar_prefetch=1,
            grid=(steps,),
            in_specs=[pl.BlockSpec(block, index) for block, index, part in arrays for _ in part],
            out_specs=pl.BlockSpec(block, index),
        ),
        out_shape=jax.ShapeDtypeStruct(shape, F32),
        compiler_params=pltpu.CompilerParams(vmem_limit_bytes=48 * MIB),
        cost_estimate=COST,
        name=name,
    )(meta, *flat)


def rows_of(part, tiles):
    return lambda i, *_: (jnp.clip(i - part * tiles, 0, tiles - 1), 0)


def finish_out(meta, parts):
    rows, cols = parts[0][0].shape
    tile, tiles = 256, rows // 256
    block = (tile, cols)

    def index(i, meta_ref):
        return ((i // (2 * tiles) ^ meta_ref[0]) * 2 * tiles + i % (2 * tiles), 0)

    def fill(read, row, out_ref):
        for k in range(4):

            @pl.when(pl.program_id(0) // tiles == k)
            def _():
                out_ref[...] = read(k)

    arrays = [(block, rows_of(k, tiles), part) for k, part in enumerate(parts)]
    return assemble("out_grad", meta, arrays, 4 * tiles, ((4 * rows, cols), block, index), fill)


def finish_in(meta, parts):
    rows, cols = parts[0][0].shape
    tile, tiles = 256, rows // 256

    def fill(read, row, out_ref):
        for k in range(2):

            @pl.when(pl.program_id(0) // tiles == k)
            def _():
                mine, other = read(k), read(2 + k)
                out_ref[:, :cols] = jnp.where(row == 0, mine, other)
                out_ref[:, cols:] = jnp.where(row == 0, other, mine)

    arrays = [((tile, cols), rows_of(k % 2, tiles), part) for k, part in enumerate(parts)]
    out = ((2 * rows, 2 * cols), (tile, 2 * cols), tiled)
    return assemble("in_grad", meta, arrays, 2 * tiles, out, fill)


def finish_qkv(meta, parts):
    feats, tile = parts[0][0].shape[1], 256
    blocks = [(2 * HS, tile), (HS, tile)] * 2

    def fill(read, row, out_ref):
        mine, other = (jnp.concatenate([read(k), read(k + 1)], 0).T for k in (0, 2))
        out_ref[:, 0, :] = jnp.where(row == 0, mine, other)
        out_ref[:, 1, :] = jnp.where(row == 0, other, mine)

    arrays = [(block, lambda i, *_: (0, i), part) for block, part in zip(blocks, parts, strict=True)]
    out = ((feats, 2, 3 * HS), (tile, 2, 3 * HS), lambda i, *_: (i, 0, 0))
    return assemble("qkv_grad", meta, arrays, feats // tile, out, fill)


def finish_dense(meta, parts):
    feats = parts[0][0].shape[1]

    def fill(read, row, out_ref):
        out_ref[row] = read(0)
        out_ref[1 - row] = read(1)

    arrays = [((HS, feats), lambda *_: (1, 0), part) for part in parts]
    out = ((2, HS, feats), (2, HS, feats), lambda *_: (0, 0, 0))
    return assemble("dense_grad", meta, arrays, 1, out, fill)


class Names:
    def __getattr__(self, name):
        return name


def is_name(value):
    return isinstance(value, (str, tuple))


class Beats:
    def __init__(self):
        self.env, self.tasks, self.flying = {}, [], []
        self.now, self.token = 0, jnp.zeros((8, LANES), F32)
        self.last, self.new = self.token, []
        self.line = Line()

    def compute(self, beat, names, fn, *inputs, top=False):
        self.tasks.append((beat, inputs, names, (fn, None) if top else fn))

    def send(self, beat, name, fn, source, beats=1):
        self.tasks.append((beat, (source,), name, (fn, beats)))

    def put(self, name, value):
        self.env[name] = value
        self.new.append(name)

    def run(self):
        while self.tasks or self.flying or self.line.busy:
            if self.now > 20 + 8 * self.line.count:
                raise ValueError([task[:3] for task in self.tasks])
            self.line.beat(self)
            for task in [t for t in self.tasks if isinstance(t[3], tuple)] + self.tasks[:]:
                beat, inputs, names, fn = task
                if not any(task is t for t in self.tasks):
                    continue
                if beat > self.now or any(is_name(i) and i not in self.env for i in inputs):
                    continue
                self.tasks = [t for t in self.tasks if t is not task]
                values = [self.env[i] if is_name(i) else i for i in inputs]
                if isinstance(fn, tuple) and fn[1] is None:
                    self.do(names, fn[0], *values)
                elif isinstance(fn, tuple):
                    fn, beats = fn
                    value = fn(tie(values[0], self.token))
                    if beats:
                        self.flying.append((self.now + beats, names, value))
                    else:
                        self.env[names] = value
                else:
                    self.do(names, fn, *values)
            self.tick()

    def do(self, names, fn, first, *rest):
        outs = fn(tie(first, self.last), *rest)
        for name, value in [(names, outs)] if is_name(names) else zip(names, outs, strict=True):
            self.put(name, value)
        self.last = jax.tree.leaves(outs)[0]
        return outs

    def tick(self):
        self.now += 1
        for due, name, value in self.flying:
            if due <= self.now:
                self.put(name, value)
        self.flying = [f for f in self.flying if f[0] > self.now]
        names = list(dict.fromkeys(n for n in self.new if n in self.env))
        values = lax.optimization_barrier((self.token, *[self.env[n] for n in names]))
        self.token = self.last = values[0]
        self.env.update(zip(names, values[1:], strict=True))
        self.new = []


class Line:
    def __init__(self):
        self.count, self.place = lax.axis_size("dp"), lax.axis_index("dp")
        self.mid = self.count // 2
        self.queue, self.going = [], []

    @property
    def busy(self):
        return bool(self.queue or self.going)

    def enter(self, *names):
        self.queue += names

    def on(self, *places):
        return (self.place == places[0]) | (self.place == places[1])

    def pairs(self, step):
        n, mid = self.count, self.mid
        if step < mid - 1:
            return [(step, step + 1), (n - 1 - step, n - 2 - step)]
        if step == mid - 1:
            return [(mid - 1, mid), (mid, mid - 1)]
        step -= mid
        return [(mid - 1 - step, mid - 2 - step), (mid + step, mid + 1 + step)]

    def beat(self, beats):
        env, mid, steps = beats.env, self.mid, 2 * self.mid - 1
        later, outward = [], {}
        for name, step in self.going:
            got, value = (name, step), (name, "held")
            if step + 1 == steps:
                src = self.pairs(step)
                held, arrived = env[value], env[got]
                env[name, "sum"] = jnp.where(self.on(src[0][1], src[1][1]), arrived, held)
                env[name, "parts"] = self.on(src[0][1], src[1][1]), arrived, held
            else:
                later.append((name, step + 1))
        starting = []
        if self.queue and self.queue[0] in env and self.queue[0] != "small":
            starting = [self.queue.pop(0)]
            env[starting[0], "held"] = env[starting[0]]
        small = [n for n in self.queue if n == "small" and n in env]
        for n in small:
            self.queue.remove(n)
            env[n, "held"] = env[n]
            starting.append(n)
        moving = [(n, 0) for n in starting] + later

        def update(name, step):
            if step == 0:
                return (lambda v: v), [(name, "held")]
            inputs = [(name, "held"), (name, step - 1)]
            if step <= mid:
                return add_low, inputs
            src = self.pairs(step - 1)
            return choose(self.on(src[0][1], src[1][1])), inputs

        for name, step in sorted(moving, key=lambda m: (m[1] != mid - 1, m[1] < mid)):
            fn, inputs = update(name, step)
            values = [env[i] for i in inputs]
            if step >= mid:
                match = [
                    m
                    for m in moving
                    if m[1] == 2 * mid - 2 - step and env[m[0]].shape == env[name].shape and m not in outward
                ]
                if match:
                    inner = match[0]
                    outward[inner] = (name, step)
                    continue
            if step < mid - 1 and (name, step) in outward:
                continue
            if step:
                beats.do((name, "held"), fn, *values)
            self.send(beats, self.pairs(step), (name, "held"), [(name, step)])
        for (name, step), (far, far_step) in outward.items():
            fn, inputs = update(name, step)
            if step:
                beats.do((name, "held"), fn, *[env[i] for i in inputs])
            inputs = update(far, far_step)[1]
            outer = self.on(step, self.count - 1 - step)
            if far_step > mid:
                gets = self.on(*[pair[1] for pair in self.pairs(far_step - 1)])
                beats.do((far, "held"), choose(gets), *[env[i] for i in inputs])
                beats.do((far, "held"), choose(outer), env[far, "held"], env[name, "held"])
            else:
                add = choose_or_add(outer)
                beats.do((far, "held"), add, env[name, "held"], *[env[i] for i in inputs])
            self.send(
                beats,
                self.pairs(step) + self.pairs(far_step),
                (far, "held"),
                [(name, step), (far, far_step)],
            )
        self.going = moving

    def send(self, beats, pairs, source, gets):
        value = lax.ppermute(tie(beats.env[source], beats.token), "dp", pairs)
        for name, step in gets:
            beats.flying.append((beats.now + 1, (name, step), value))


def per_device(
    residual_in,
    attn_gain,
    attn_shift,
    mlp_gain,
    mlp_shift,
    qkv_weight,
    qkv_bias,
    dense_weight,
    dense_bias,
    in_weight,
    in_bias,
    out_weight,
    out_bias,
    cotangent,
):
    row, col = lax.axis_index("row"), lax.axis_index("col")
    rows, feats = residual_in.shape
    slots, width = lax.axis_size("col"), 2 * feats
    units = in_weight.shape[1] // 2
    other = 1 - row
    plan = Beats()
    env, compute, send, n = plan.env, plan.compute, plan.send, Names()

    def summed(name):
        return name, n.sum


    def below(*parts):
        return jnp.concatenate(parts, 0)

    def part(lo, hi):
        return lambda v: lax.slice_in_dim(v, lo, hi)

    def share(beat, name, fn, source, *needs):
        compute_free = (beat, (source, *needs), name, (fn, 0))
        plan.tasks.append(compute_free)

    env.update(res=residual_in, cot=cotangent)
    env[n.gx] = jnp.stack([attn_gain, attn_shift, mlp_gain, mlp_shift])

    send(0, n.gy, swap_row, n.gx)
    send(0, n.res_x, swap_row, n.res)
    send(0, n.res_y, swap_y, n.res)
    send(0, n.res_c, swap_core, n.res)
    mid = feats // 2
    pick = lax.dynamic_slice
    compute(0, n.in_sent0, lambda w: pick(w, (0, other * units), (mid, units)), in_weight)
    compute(0, n.wx, lambda w: half(w, 1, row), in_weight)
    compute(0, n.ox, lambda w: half(w, 0, row), out_weight)
    compute(0, n.in_sent1, lambda w: pick(w, (mid, other * units), (mid, units)), in_weight)

    compute(0, [n.cos, n.low, n.high], lambda _: rotary_tables(slots * rows), n.gx)

    send(1, n.wy0, swap_row, n.in_sent0)
    send(1, n.res_xy, swap_y, n.res_x)
    send(1, n.res_xc, swap_core, n.res_x)
    send(1, n.res_yc, swap_core, n.res_y)
    compute(1, n.norm0, lambda *a: norm_call(col, 0, *a), n.res, n.res_x, n.gx, n.gy)
    for i in range(2):
        at = other * units + i * (units // 2)
        compute(1, (n.oy_sent, i), lambda w, at=at: pick(w, (at, 0), (units // 2, feats)), out_weight)
    compute(1, n.qx, lambda w: lax.dynamic_index_in_dim(w, row, 1, False), qkv_weight)
    compute(1, n.dense_sent, lambda w: lax.dynamic_index_in_dim(w, other, 0, False), dense_weight)
    compute(1, n.dx, lambda w: lax.dynamic_index_in_dim(w, row, 0, False), dense_weight)

    send(2, n.wy1, swap_row, n.in_sent1)
    send(2, n.res_xyc, swap_core, n.res_xy, 0)

    def gather_col(value):
        return lax.all_gather(value, "col", axis=0, tiled=True)

    share(2, n.g, gather_col, n.cot)

    def norm_rest(res_c, res_xc, res_y, res_xy, res_yc, res_xyc, gx, gy, before):
        before = norm_call(col, 1, res_c, res_xc, gx, gy, *before)
        before = norm_call(col, 2, res_y, res_xy, gx, gy, *before)
        return norm_call(col, 3, res_yc, res_xyc, gx, gy, *before)

    compute(
        2,
        [n.ax, n.ay, n.mx, n.my],
        norm_rest,
        *[n.res_c, n.res_xc, n.res_y, n.res_xy, n.res_yc, n.res_xyc, n.gx, n.gy, n.norm0],
    )

    send(3, n.cot_x, swap_row, n.cot)
    in_bias_mine = lax.dynamic_slice_in_dim(in_bias, row * units, units, 0)
    compute(3, [n.active, n.slope], pre_call, n.mx, n.my, n.wx, n.wy0, n.wy1, in_bias_mine)

    def grads(beat, names, cuts, *inputs):
        compute(beat, names, lambda *a: weight_grad(cuts, *a), *inputs)

    two = [units // 2] * 2
    half_units = [units // 2]
    grads(3, [n.out_own0], half_units, n.active, n.g)
    z = 4
    for i in range(2):
        send(z + i, (n.oy, i), swap_row, (n.oy_sent, i))
    oy = [(n.oy, 0), (n.oy, 1)]
    compute(z, [n.out_own1], lambda a, g: weight_grad(half_units, (a, units // 2), g), n.active, n.g)
    share(z, n.h, gather_col, n.cot_x)
    compute(z, n.x_near, below, n.res, n.res_y)
    compute(z, n.y_near, below, n.res_x, n.res_xy)
    compute(z, n.x_far, below, n.res_c, n.res_yc)
    compute(z, n.y_far, below, n.res_xc, n.res_xyc)
    grads(z + 1, [n.out_oth0, n.out_oth1], two, n.active, n.h)
    compute(z + 2, [n.pre_grad, n.in_bias_sum], pre_grad_call, n.g, n.h, n.ox, *oy, n.slope)
    two = [feats // 2] * 2
    grads(z + 3, [n.in_own0, n.in_own1], two, n.mx, n.pre_grad)
    grads(z + 3, [n.in_oth0, n.in_oth1], two, n.my, n.pre_grad)
    cut = 5 * feats // 8
    for i, (lo, hi) in enumerate(((0, cut), (cut, feats))):
        sent = (n.qy_sent, i)
        compute(2, sent, lambda w, lo=lo, hi=hi: lax.dynamic_index_in_dim(w[lo:hi], other, 1, False), qkv_weight)
        send(z + 2 + i, (n.qy, i), swap_row, sent)
    send(z + 3, n.dy, swap_row, n.dense_sent)
    compute(z + 4, n.qy, below, (n.qy, 0), (n.qy, 1))
    qkv_bias_mine = lax.dynamic_index_in_dim(qkv_bias, row, 0, False)
    compute(
        z + 4,
        [n.query, n.key, n.value],
        packed_call,
        *[n.ax, n.ay, n.qx, n.qy, qkv_bias_mine, n.cos, n.low, n.high],
    )
    compute(
        z + 4,
        n.attended_grad,
        lambda g, h, dx, dy: (dot(g, dx, NT) + dot(h, dy, NT)).astype(BF),
        *[n.g, n.h, n.dx, n.dy],
    )
    compute(
        z + 5,
        [n.packed_grad, n.attended, n.qkv_bias_sum],
        lambda *a: attention(slots, *a),
        *[n.query, n.key, n.value, n.attended_grad, n.cos, n.low, n.high],
    )
    cuts = [2 * HS, 2 * HS]
    grads(z + 6, [n.att_own0, n.att_own1], cuts, n.packed_grad, n.ax, n.attended, n.g)
    grads(z + 6, [n.att_oth0, n.att_oth1], cuts, n.packed_grad, n.ay, n.attended, n.h)

    send(z + 4, n.in_oth0_x, swap_row, n.in_oth0)
    send(z + 5, n.in_oth1_x, swap_row, n.in_oth1)
    send(z + 7, n.att_oth0_x, swap_row, n.att_oth0)
    send(z + 8, n.att_oth1_x, swap_row, n.att_oth1)
    plan.line.enter(
        *(n.out_own0, n.out_own1, n.out_oth0, n.out_oth1, n.in_own0, n.in_own1, n.in_oth0_x),
        *(n.att_own0, n.att_own1, n.att_oth0_x, n.att_oth1_x, n.in_oth1_x, n.small),
    )

    def choose_part(parts):
        return choose(parts[0])(parts[2], parts[1])

    compute(z + 5, n.out_oth0_s, choose_part, (n.out_oth0, n.parts))
    compute(z + 6, n.out_oth1_s, choose_part, (n.out_oth1, n.parts))
    send(z + 6, n.out_oth0_y, swap_row, n.out_oth0_s)
    send(z + 9, n.out_oth1_y, swap_row, n.out_oth1_s)

    for beat, part, name, sums, x, y in (
        (z + 7, 1, (n.ng, n.far), n.sums_far, n.x_far, n.y_far),
        (z + 8, 0, (n.ng, n.near), n.sums_near, n.x_near, n.y_near),
    ):
        compute(
            beat,
            [name, sums],
            lambda *a, part=part: norm_grad_call(col, part, *a),
            *[x, y, n.gx, n.gy, n.packed_grad, n.pre_grad, n.qx, n.qy, n.wx, n.wy0, n.wy1],
        )
    for beat, part, name in ((z + 9, 1, (n.mixed, n.far)), (z + 10, 0, (n.mixed, n.near))):
        compute(
            beat,
            name,
            lambda *a, part=part: mixed_call(col, part, *a),
            *[n.attended, n.active, n.dx, n.dy, n.ox, *oy],
        )

    part_rows = rows // 2

    def near(a, b, *c):
        def fn(a, b, c0, c1):
            c = jnp.where(pl.program_id(0) == 0, c0, c1)
            out = a.astype(F32) + b.astype(F32) + c.astype(F32)
            return [out[:, feats:].astype(BF), out[:, :feats]]

        return rowwise(fn, rows, [(feats, BF), (feats, F32)], a, b, *[(v, None) for v in c])

    def far_sum(i):
        at, outs = rows + i * part_rows, [(width, BF)]
        return lambda a, b: rowwise(plain_add, part_rows, outs, (a, at), (b, at))[0]

    def scatter(beat, name):
        far, mine, got = [(name, i) for i in (n.far, n.near, n.core)]
        send(beat, got, swap_core, far)
        got_y = [(name, n.near, i) for i in range(2)]
        for i in range(2):
            far_y = (name, n.far, i)
            compute(beat + 1, far_y, far_sum(i), mine, got, top=i == 0)
            send(beat + 1 + i, got_y[i], swap_y, far_y)
        compute(beat + 3, [(name, n.sent), (name, n.keep)], near, mine, got, *got_y, top=True)
        send(beat + 3, (name, n.got), swap_row, (name, n.sent))

    scatter(z + 8, n.ng)
    scatter(z + 10, n.mixed)
    compute(
        z + 14,
        n.block_out,
        lambda a, xg, res, b, c: (res.astype(F32) + a + xg.astype(F32) + b + c).astype(BF),
        *[(n.mixed, n.keep), (n.mixed, n.got), n.res, dense_bias, out_bias],
    )

    def own_norm(res, res_x):
        x, y = res.astype(F32), res_x.astype(F32)
        average = (jnp.sum(x, 1, keepdims=True) + jnp.sum(y, 1, keepdims=True)) / width
        squares = (jnp.sum(x * x, 1, keepdims=True) + jnp.sum(y * y, 1, keepdims=True)) / width
        scale = lax.rsqrt(squares - average * average + EPSILON)
        return (x - average) * scale, scale

    def token_sums(keep, xg, res, res_x):
        normed, scale = own_norm(res, res_x)
        grad = keep + xg.astype(F32)
        return jnp.stack([jnp.sum(grad, 1), jnp.sum(grad * normed, 1)])

    compute(z + 12, n.tok, token_sums, (n.ng, n.keep), (n.ng, n.got), n.res, n.res_x)
    send(z + 12, n.tok_x, swap_row, n.tok)

    def finish_input(keep, xg, res, res_x, cot, tok, tok_x):
        normed, scale = own_norm(res, res_x)
        tok = (tok + tok_x) / width
        grad = keep + xg.astype(F32)
        return cot.astype(F32) + scale * (grad - tok[0][:, None] - normed * tok[1][:, None])

    rest = [n.res, n.res_x, n.cot, n.tok, n.tok_x]
    compute(
        z + 13, n.input_grad, finish_input, (n.ng, n.keep), (n.ng, n.got), *rest
    )

    def small_all(near, far, cot, qkv_bias_sum, in_bias_sum):
        bias_sum = jnp.pad(jnp.sum(cot, 0, dtype=F32), (0, feats))
        parts = [(near + far).reshape(-1), bias_sum, qkv_bias_sum.reshape(-1), in_bias_sum.reshape(-1)]
        return jnp.concatenate(parts)

    def take(parts):
        return jnp.where(parts[0], parts[1], parts[2])

    compute(z + 8, n.small, small_all, n.sums_near, n.sums_far, n.cot, n.qkv_bias_sum, n.in_bias_sum)
    compute(z + 12, n.small_s, take, (n.small, n.parts), top=True)
    send(z + 12, n.small_x, swap_row, n.small_s)

    def by_feature(mine, got):
        mine, got = (v[: 5 * width].reshape(5, width) for v in (mine, got))
        return mine[:, :feats] + got[:, feats:]

    compute(z + 13, n.small0, by_feature, n.small_s, n.small_x)
    send(z + 13, n.small0_c, swap_core, n.small0, 0)
    compute(z + 13, n.small1, jnp.add, n.small0, n.small0_c)
    send(z + 13, n.small1_y, swap_y, n.small1, 0)
    compute(z + 13, n.small2, jnp.add, n.small1, n.small1_y)

    def finish(beat, name, fn, *sources):
        def step(*sources):
            flag = next(v[0] for v in sources if isinstance(v, tuple))
            arrays = [v[1:] if isinstance(v, tuple) else (v,) for v in sources]
            return fn(jnp.stack([row, flag.astype(jnp.int32)]), arrays)

        compute(beat, name, step, *sources)

    def done(*names):
        return [(v, n.parts) for v in names]

    finish(z + 12, n.out_weight_grad, finish_out, *done(n.out_own0, n.out_own1), n.out_oth0_y, n.out_oth1_y)
    att = done(n.att_own0, n.att_own1, n.att_oth0_x, n.att_oth1_x)
    finish(z + 13, n.qkv_weight_grad, finish_qkv, *att)
    finish(z + 13, n.dense_weight_grad, finish_dense, att[1], att[3])
    finish(
        z + 14, n.in_weight_grad, finish_in, *done(n.in_own0, n.in_own1, n.in_oth0_x, n.in_oth1_x)
    )
    plan.run()
    def in_order(mine, got):
        return jnp.where(row == 0, jnp.concatenate([mine, got]), jnp.concatenate([got, mine]))

    by_feature = env[n.small2]
    by_col, by_col_got = (env[name][5 * width :] for name in (n.small_s, n.small_x))
    qkv_bias_grad = in_order(by_col[: 3 * HS], by_col_got[: 3 * HS]).reshape(2, 3 * HS)
    in_bias_grad = in_order(by_col[3 * HS :], by_col_got[3 * HS :])
    return (
        env[n.block_out],
        env[n.input_grad],
        by_feature[0],
        by_feature[1],
        by_feature[2],
        by_feature[3],
        env[n.qkv_weight_grad],
        qkv_bias_grad,
        env[n.dense_weight_grad],
        by_feature[4],
        env[n.in_weight_grad],
        in_bias_grad,
        env[n.out_weight_grad],
        by_feature[4],
    )


def solution(mesh):
    in_specs = (
        P(("dp", "col"), "row"),
        P("row"),
        P("row"),
        P("row"),
        P("row"),
        P("row", "col", None),
        P("col", None),
        P("col", None, "row"),
        P("row"),
        P("row", "col"),
        P("col"),
        P("col", "row"),
        P("row"),
        P(("dp", "col"), "row"),
    )
    out_specs = (
        P(("dp", "col"), "row"),
        P(("dp", "col"), "row"),
        P("row"),
        P("row"),
        P("row"),
        P("row"),
        P("row", "col", None),
        P("col", None),
        P("col", None, "row"),
        P("row"),
        P("row", "col"),
        P("col"),
        P("col", "row"),
        P("row"),
    )
    return jax.shard_map(
        per_device, mesh=mesh, in_specs=in_specs, out_specs=out_specs, check_vma=False
    )
```

```python
import math

import jax
import jax.numpy as jnp
from jax import lax
from jax.experimental import pallas as pl
from jax.experimental.pallas import tpu as pltpu
from jax.sharding import PartitionSpec as P

HS = 256
ROT = 64
LENGTH = 2048
LANES = 128
EPSILON = 1e-05
ROPE_BASE = 10000.0
NEGATIVE = -1e30
BF = jnp.bfloat16
F32 = jnp.float32
NN, NT, TN = ((1,), (0,)), ((1,), (1,)), ((0,), (0,))
MIB = 2**20
COST = pl.CostEstimate(flops=0, bytes_accessed=0, transcendentals=0)


def tie(value, *others):
    return lax.optimization_barrier((value,) + others)[0]


def swap_row(value):
    return lax.ppermute(value, "row", [(0, 1), (1, 0)])


def swap_col(value, bit):
    return lax.ppermute(value, "col", [(i, i ^ bit) for i in range(lax.axis_size("col"))])


def swap_y(value):
    return swap_col(value, 2)


def swap_core(value):
    return swap_col(value, 1)


def half(array, axis, index):
    size = array.shape[axis] // 2
    return lax.dynamic_slice_in_dim(array, index * size, size, axis)


def dot(a, b, dims):
    return lax.dot_general(a, b, (dims, ((), ())), preferred_element_type=F32)


def rotary_tables(tokens):
    position = (jnp.arange(tokens) % LENGTH).astype(F32)
    lane = jnp.arange(LANES)
    index = (lane % (ROT // 2)).astype(F32)
    frequency = ROPE_BASE ** (-(2.0 * index) / ROT)
    angle = position[:, None] * frequency[None, :]
    cos = jnp.where(lane < ROT, jnp.cos(angle), 1.0)
    sin = jnp.sin(angle)
    low = jnp.where(lane < ROT // 2, -sin, 0.0)
    high = jnp.where((lane >= ROT // 2) & (lane < ROT), sin, 0.0)
    return cos, low, high


def rotate(values, cos, low, high):
    first = values[:, :LANES]
    up = pltpu.roll(first, LANES - ROT // 2, 1)
    down = pltpu.roll(first, ROT // 2, 1)
    first = first * cos + up * low + down * high
    return jnp.concatenate([first, values[:, LANES:]], 1)


def tiled(i, *_):
    return (i, 0)


def fixed(*_):
    return (0, 0)


def call(kernel, name, steps, ins, outs, col=None, vmem=28, tile=None):
    def block(shape, index, rows=None):
        rows = rows or (shape[0] if index is fixed else tile or shape[0] // steps)
        return pl.BlockSpec((rows, shape[1]), index)

    spec = pltpu.PrefetchScalarGridSpec(
        num_scalar_prefetch=0 if col is None else 1,
        grid=(steps,),
        in_specs=[block(a.shape, index) for a, index in ins],
        out_specs=tuple(block(shape, index, rows) for shape, _, rows, index in outs),
    )
    return pl.pallas_call(
        kernel if col is None else lambda _, *refs: kernel(*refs),
        grid_spec=spec,
        out_shape=tuple(jax.ShapeDtypeStruct(shape, dtype) for shape, dtype, _, _ in outs),
        compiler_params=pltpu.CompilerParams(vmem_limit_bytes=vmem * MIB),
        cost_estimate=COST,
        name=name,
    )(*([] if col is None else [col.reshape(1)]), *[a for a, _ in ins])


def normed_halves(x_ref, y_ref):
    x, y = x_ref[...].astype(F32), y_ref[...].astype(F32)
    width = x.shape[1] + y.shape[1]
    average = (jnp.sum(x, 1, keepdims=True) + jnp.sum(y, 1, keepdims=True)) / width
    squares = (jnp.sum(x * x, 1, keepdims=True) + jnp.sum(y * y, 1, keepdims=True)) / width
    scale = lax.rsqrt(squares - average * average + EPSILON)
    return (x - average) * scale, (y - average) * scale


def norm_kernel(x_ref, y_ref, gx_ref, gy_ref, ax_ref, ay_ref, mx_ref, my_ref):
    x, y = normed_halves(x_ref, y_ref)
    ax_ref[...] = (x * gx_ref[0:1] + gx_ref[1:2]).astype(BF)
    ay_ref[...] = (y * gy_ref[0:1] + gy_ref[1:2]).astype(BF)
    mx_ref[...] = (x * gx_ref[2:3] + gx_ref[3:4]).astype(BF)
    my_ref[...] = (y * gy_ref[2:3] + gy_ref[3:4]).astype(BF)


def norm_call(col, flip, x, y, gx, gy, *before):
    (rows, feats), tile, slots = x.shape, 256, 4
    steps = rows // tile

    def index(i, col_ref):
        return ((col_ref[0] ^ flip) * steps + i, 0)

    rest = [pl.BlockSpec(memory_space=pl.ANY)] * len(before)
    block = pl.BlockSpec((tile, feats), tiled)
    whole = pl.BlockSpec(gx.shape, fixed)
    return pl.pallas_call(
        lambda _, x, y, gx, gy, *refs: norm_kernel(x, y, gx, gy, *refs[len(before) :]),
        grid_spec=pltpu.PrefetchScalarGridSpec(
            num_scalar_prefetch=1,
            grid=(steps,),
            in_specs=[block, block, whole, whole] + rest,
            out_specs=(pl.BlockSpec((tile, feats), index),) * 4,
        ),
        out_shape=(jax.ShapeDtypeStruct((slots * rows, feats), BF),) * 4,
        input_output_aliases={5 + i: i for i in range(len(before))},
        compiler_params=pltpu.CompilerParams(vmem_limit_bytes=58 * MIB),
        cost_estimate=COST,
        name="norm",
    )(col.reshape(1), x, y, gx, gy, *before)


def pre_kernel(x_ref, y_ref, wx_ref, wy0_ref, wy1_ref, bias_ref, active_ref, slope_ref):
    mid, part = wy0_ref.shape[0], wx_ref.shape[1]
    for start in range(0, wx_ref.shape[1], part):
        at = slice(start, start + part)
        u = dot(x_ref[...], wx_ref[:, at], NN) + bias_ref[:, at]
        u = u + dot(y_ref[:, :mid], wy0_ref[:, at], NN) + dot(y_ref[:, mid:], wy1_ref[:, at], NN)
        phi = 0.5 * (1.0 + lax.erf(u * 2.0**-0.5))
        bell = jnp.exp(-0.5 * u * u)
        active_ref[:, at] = (u * phi).astype(BF)
        slope_ref[:, at] = (phi + u * bell * (2.0 * math.pi) ** (-0.5)).astype(BF)


def pre_call(x, y, wx, wy0, wy1, bias):
    tokens, tile, units = x.shape[0], 256, wx.shape[1]
    return call(
        pre_kernel,
        "pre_act",
        tokens // tile,
        [(x, tiled), (y, tiled), (wx, fixed), (wy0, fixed), (wy1, fixed), (bias.reshape(1, -1), fixed)],
        [((tokens, units), BF, tile, tiled)] * 2,
        vmem=58,
    )


def rowwise(fn, rows, outs, *ins, flag=None, vmem=20, whole=None, skip=0, before=()):
    tile = 256
    ins = [i if isinstance(i, tuple) else (i, 0) for i in ins]
    flags = [] if flag is None else [flag.astype(jnp.int32).reshape(1)]

    def at(first):
        return fixed if first is None else lambda i, *_: (i + first // tile, 0)

    def kernel(*refs):
        values = [ref[0] != 0 for ref in refs[: len(flags)]]
        refs = refs[len(flags) :]
        results = fn(*values, *[ref[...] for ref in refs[: len(ins)]])
        for ref, result in zip(refs[len(ins) + len(before) :], results, strict=True):
            ref[...] = result

    first_in = len(flags) + len(ins)
    return pl.pallas_call(
        kernel,
        grid_spec=pltpu.PrefetchScalarGridSpec(
            num_scalar_prefetch=len(flags),
            grid=(rows // tile,),
            in_specs=[pl.BlockSpec((tile, a.shape[1]), at(first)) for a, first in ins]
            + [pl.BlockSpec(memory_space=pl.ANY)] * len(before),
            out_specs=tuple(pl.BlockSpec((tile, cols), at(skip)) for cols, _ in outs),
        ),
        out_shape=tuple(jax.ShapeDtypeStruct((whole or rows, cols), dtype) for cols, dtype in outs),
        input_output_aliases={first_in + i: i for i in range(len(before))},
        compiler_params=pltpu.CompilerParams(vmem_limit_bytes=vmem * MIB),
        cost_estimate=COST,
        name="rowwise",
    )(*flags, *[a for a, _ in ins], *before)


def plain_add(a, b):
    return [(a.astype(F32) + b.astype(F32)).astype(BF)]


def add_low(a, b):
    return (a.astype(F32) + b.astype(F32)).astype(a.dtype)


def choose(flag):
    def fn(held, arrived):
        if held.ndim == 1:
            return jnp.where(flag, arrived, held)
        outs = [(held.shape[1], BF)]
        return rowwise(lambda f, h, a: [jnp.where(f, a, h)], held.shape[0], outs, held, arrived, flag=flag)[0]

    return fn


def choose_or_add(flag):
    return lambda value, a, b: jnp.where(flag, value, add_low(a, b))


def weight_grad(cuts, a, b, last_a=None, last_b=None, vmem=20):
    tokens, cols, tile = b.shape[0], b.shape[1], 256
    own = sum(cuts) // tile if last_a is None else a.shape[1] // tile
    skip = 0
    if isinstance(a, tuple):
        a, skip = a[0], a[1] // tile
    first = [sum(cuts[:i]) // tile for i in range(len(cuts) + 1)]

    def kernel(*refs):
        step = pl.program_id(0)

        def store(out):
            for start, end, ref in zip(first[:-1], first[1:], refs[-len(cuts) :], strict=True):

                @pl.when((step >= start) & (step < end))
                def _():
                    ref[...] = out

        if last_a is None:
            store(dot(refs[0][...], refs[1][...], TN).astype(BF))
            return

        @pl.when(step < own)
        def _():
            store(dot(refs[0][...], refs[1][...], TN).astype(BF))

        @pl.when(step >= own)
        def _():
            store(dot(refs[2][...], refs[3][...], TN).astype(BF))

    def index(start, end):
        return lambda i: (jnp.clip(i - start, 0, end - start - 1), 0)

    ins = [a, b] if last_a is None else [a, b, last_a, last_b]
    specs = [
        pl.BlockSpec((tokens, tile), lambda i: (0, jnp.minimum(i, own - 1) + skip)),
        pl.BlockSpec(b.shape, fixed),
        pl.BlockSpec((tokens, tile), fixed),
        pl.BlockSpec(b.shape, fixed),
    ]
    return pl.pallas_call(
        kernel,
        grid=(first[-1],),
        out_shape=tuple(jax.ShapeDtypeStruct((size, cols), BF) for size in cuts),
        in_specs=specs[: len(ins)],
        out_specs=tuple(
            pl.BlockSpec((tile, cols), index(s, e)) for s, e in zip(first[:-1], first[1:], strict=True)
        ),
        compiler_params=pltpu.CompilerParams(vmem_limit_bytes=vmem * MIB),
        cost_estimate=COST,
        name="weight_grad",
    )(*ins)


def pre_grad_kernel(gx_ref, gy_ref, wx_ref, wy0_ref, wy1_ref, slope_ref, out_ref, sum_ref):
    @pl.when(pl.program_id(0) == 0)
    def _():
        sum_ref[...] = jnp.zeros_like(sum_ref)

    mid = wy0_ref.shape[0]
    for i, wy_ref in enumerate((wy0_ref, wy1_ref)):
        at = slice(i * mid, (i + 1) * mid)
        u = dot(gx_ref[...], wx_ref[at, :], NT) + dot(gy_ref[...], wy_ref[...], NT)
        low = (u * slope_ref[:, at].astype(F32)).astype(BF)
        out_ref[:, at] = low
        sum_ref[:, at] += jnp.sum(low.astype(F32), 0, keepdims=True)


def pre_grad_call(gx, gy, wx, wy0, wy1, slope):
    tokens, tile, units = gx.shape[0], 512, wx.shape[0]
    return call(
        pre_grad_kernel,
        "pre_grad",
        tokens // tile,
        [(gx, tiled), (gy, tiled), (wx, fixed), (wy0, fixed), (wy1, fixed), (slope, tiled)],
        [((tokens, units), BF, tile, tiled), ((1, units), F32, 1, fixed)],
    )


def packed_kernel(x_ref, y_ref, wx_ref, wy_ref, bias_ref, cos_ref, low_ref, high_ref, q_ref, k_ref, v_ref):
    out = dot(x_ref[...], wx_ref[...], NN) + dot(y_ref[...], wy_ref[...], NN) + bias_ref[...]
    tables = cos_ref[...], low_ref[...], high_ref[...]
    q_ref[...] = rotate(out[:, :HS], *tables).astype(BF)
    k_ref[...] = rotate(out[:, HS : 2 * HS], *tables).astype(BF)
    v_ref[...] = out[:, 2 * HS :].astype(BF)


def packed_call(x, y, wx, wy, bias, *tables):
    tokens, tile = x.shape[0], 512
    return call(
        packed_kernel,
        "packed",
        tokens // tile,
        [(x, tiled), (y, tiled), (wx, fixed), (wy, fixed), (bias.reshape(1, -1), fixed)]
        + [(t, tiled) for t in tables],
        [((tokens, HS), BF, tile, tiled)] * 3,
    )


def attention_kernel(
    q_ref, k_ref, v_ref, g_ref, cos_ref, low_ref, high_ref, o_ref, out_ref, sum_ref, dk_acc, dv_acc
):
    slots, rows, _ = q_ref.shape
    scale = HS ** (-0.5)
    mask = lax.broadcasted_iota(jnp.int32, (rows, rows), 1) <= lax.broadcasted_iota(
        jnp.int32, (rows, rows), 0
    )
    total_sum = [jnp.zeros((1, HS), F32) for _ in range(3)]

    def unrotate(values, at):
        return rotate(values, cos_ref[at], -low_ref[at], -high_ref[at]).astype(BF)

    for i in range(slots):
        q, g = q_ref[i], g_ref[i]
        scores = []
        for j in range(i + 1):
            s = dot(q, k_ref[j], NT) * scale
            scores.append(jnp.where(mask, s, NEGATIVE) if j == i else s)
        top = scores[0].max(-1, keepdims=True)
        for s in scores[1:]:
            top = jnp.maximum(top, s.max(-1, keepdims=True))
        exps = [jnp.exp(s - top) for s in scores]
        inv = 1.0 / sum(e.sum(-1, keepdims=True) for e in exps)
        probs = [e * inv for e in exps]
        out = jnp.zeros((rows, HS), F32)
        center = jnp.zeros((rows, 1), F32)
        prob_grads = []
        for j in range(i + 1):
            low = probs[j].astype(BF)
            v = v_ref[j]
            out = out + dot(low, v, NN)
            pg = dot(g, v, NT)
            center = center + (probs[j] * pg).sum(-1, keepdims=True)
            prob_grads.append(pg)
            dv = dot(low, g, TN)
            if j == i:
                dv_acc[j] = dv
            else:
                dv_acc[j] += dv
        o_ref[i] = out.astype(BF)
        dq = jnp.zeros((rows, HS), F32)
        for j in range(i + 1):
            sg = (probs[j] * (prob_grads[j] - center)).astype(BF)
            dq = dq + dot(sg, k_ref[j], NN)
            dk = dot(sg, q, TN)
            if j == i:
                dk_acc[j] = dk
            else:
                dk_acc[j] += dk
        dq = unrotate(dq * scale, i)
        out_ref[i, :, 0:HS] = dq
        total_sum[0] = total_sum[0] + jnp.sum(dq.astype(F32), 0, keepdims=True)
    for j in range(slots):
        dk = unrotate(dk_acc[j] * scale, j)
        dv = dv_acc[j].astype(BF)
        out_ref[j, :, HS : 2 * HS] = dk
        out_ref[j, :, 2 * HS :] = dv
        total_sum[1] = total_sum[1] + jnp.sum(dk.astype(F32), 0, keepdims=True)
        total_sum[2] = total_sum[2] + jnp.sum(dv.astype(F32), 0, keepdims=True)
    for i in range(3):
        sum_ref[:, i * HS : (i + 1) * HS] = total_sum[i]


def attention(slots, q, k, v, g, cos, low, high):
    tokens = q.shape[0]
    rows = tokens // slots
    vmem = pl.BlockSpec(memory_space=pltpu.VMEM)
    attended, packed_grad, sums = pl.pallas_call(
        attention_kernel,
        out_shape=(
            jax.ShapeDtypeStruct((slots, rows, HS), BF),
            jax.ShapeDtypeStruct((slots, rows, 3 * HS), BF),
            jax.ShapeDtypeStruct((1, 3 * HS), F32),
        ),
        in_specs=[vmem] * 7,
        out_specs=(vmem,) * 3,
        scratch_shapes=[pltpu.VMEM((slots, rows, HS), F32)] * 2,
        compiler_params=pltpu.CompilerParams(vmem_limit_bytes=48 * MIB),
        cost_estimate=COST,
        name="attention",
    )(*[a.reshape(slots, rows, a.shape[1]) for a in (q, k, v, g, cos, low, high)])
    return packed_grad.reshape(tokens, 3 * HS), attended.reshape(tokens, HS), sums


def mixed_kernel(a_ref, b_ref, dx_ref, dy_ref, wx_ref, wy0_ref, wy1_ref, out_ref):
    feats, mid = dx_ref.shape[1], wy0_ref.shape[0]
    a, b = a_ref[...], b_ref[...]
    out_ref[:, :feats] = (dot(a, dx_ref[...], NN) + dot(b, wx_ref[...], NN)).astype(BF)
    y = dot(a, dy_ref[...], NN) + dot(b[:, :mid], wy0_ref[...], NN) + dot(b[:, mid:], wy1_ref[...], NN)
    out_ref[:, feats:] = y.astype(BF)


def mixed_call(col, part, attended, active, dx, dy, *weights):
    tokens, tile, width = attended.shape[0] // 2, 256, dx.shape[1] + dy.shape[1]
    steps = tokens // tile
    each = steps // 2

    def order(i, col_ref):
        return ((col_ref[0] ^ part ^ (2 * (i // each))) * each + i % each, 0)

    ins = [(attended, order), (active, order)] + [(w, fixed) for w in (dx, dy, *weights)]
    outs = [((tokens, width), BF, tile, tiled)]
    return call(mixed_kernel, "mixed", steps, ins, outs, col, tile=tile)[0]


def norm_grad_kernel(
    x_ref, y_ref, gx_ref, gy_ref, p_ref, u_ref, qx_ref, qy_ref, wx_ref, wy0_ref, wy1_ref, out_ref, sum_ref
):
    feats, mid = x_ref.shape[1], wy0_ref.shape[0]

    @pl.when(pl.program_id(0) == 0)
    def _():
        sum_ref[...] = jnp.zeros_like(sum_ref)

    normed = normed_halves(x_ref, y_ref)
    p, u = p_ref[...], u_ref[...]
    for start in range(0, 2 * feats, mid):
        side, lo = divmod(start, feats)
        at, part = slice(start, start + mid), slice(lo, lo + mid)
        q = (qx_ref, qy_ref)[side][part, :]
        w = wx_ref[part, :] if side == 0 else (wy0_ref, wy1_ref)[lo // mid][...]
        gains = (gx_ref, gy_ref)[side][:, part]
        n = normed[side][:, part]
        a, m = dot(p, q, NT), dot(u, w, NT)
        out_ref[:, at] = (a * gains[0:1] + m * gains[2:3]).astype(BF)
        sum_ref[0:1, at] += jnp.sum(a * n, 0, keepdims=True)
        sum_ref[1:2, at] += jnp.sum(a, 0, keepdims=True)
        sum_ref[2:3, at] += jnp.sum(m * n, 0, keepdims=True)
        sum_ref[3:4, at] += jnp.sum(m, 0, keepdims=True)


def norm_grad_call(col, part, x, y, gx, gy, packed_grad, pre_grad, *weights):
    tokens, tile, width = x.shape[0], 256, x.shape[1] + y.shape[1]
    steps = tokens // tile
    each = steps // 2

    def order(i, col_ref):
        return ((col_ref[0] ^ part ^ (2 * (i // each))) * each + i % each, 0)

    ins = [(x, tiled), (y, tiled), (gx, fixed), (gy, fixed), (packed_grad, order), (pre_grad, order)]
    return call(
        norm_grad_kernel,
        "norm_grad",
        steps,
        ins + [(w, fixed) for w in weights],
        [((tokens, width), BF, tile, tiled), ((4, width), F32, 4, fixed)],
        col,
        vmem=58,
        tile=tile,
    )


def assemble(name, meta, arrays, steps, out, fill, before=None):
    flat = [a for _, _, part in arrays for a in part]
    rest = [] if before is None else [before]
    shape, block, index = out

    def kernel(meta_ref, *refs):
        at = iter(refs[:-1])
        parts = [[next(at) for _ in part] for _, _, part in arrays]

        def read(i):
            values = [ref[...] for ref in parts[i]]
            value = values[0] if len(values) == 1 else jnp.where(meta_ref[1] != 0, *values)
            return value.astype(F32)

        fill(read, meta_ref[0], refs[-1])

    return pl.pallas_call(
        kernel,
        grid_spec=pltpu.PrefetchScalarGridSpec(
            num_scalar_prefetch=1,
            grid=(steps,),
            in_specs=[pl.BlockSpec(block, index) for block, index, part in arrays for _ in part]
            + [pl.BlockSpec(memory_space=pl.ANY)] * len(rest),
            out_specs=pl.BlockSpec(block, index),
        ),
        out_shape=jax.ShapeDtypeStruct(shape, F32),
        input_output_aliases={1 + len(flat): 0} if rest else {},
        compiler_params=pltpu.CompilerParams(vmem_limit_bytes=58 * MIB),
        cost_estimate=COST,
        name=name,
    )(meta, *flat, *rest)


def rows_of(part, tiles):
    return lambda i, *_: (jnp.clip(i - part * tiles, 0, tiles - 1), 0)


def finish_out(meta, parts):
    rows, cols = parts[0][0].shape
    tile, tiles = 256, rows // 256
    block = (tile, cols)

    def index(i, meta_ref):
        return ((i // (2 * tiles) ^ meta_ref[0]) * 2 * tiles + i % (2 * tiles), 0)

    def fill(read, row, out_ref):
        for k in range(4):

            @pl.when(pl.program_id(0) // tiles == k)
            def _():
                out_ref[...] = read(k)

    arrays = [(block, rows_of(k, tiles), part) for k, part in enumerate(parts)]
    return assemble("out_grad", meta, arrays, 4 * tiles, ((4 * rows, cols), block, index), fill)


def finish_in(meta, parts, before=None):
    rows, cols = parts[0][0].shape
    tile, tiles = 256, rows // 256
    skip = 0 if before is None else tiles

    def fill(read, row, out_ref):
        mine, other = read(0), read(1)
        out_ref[:, :cols] = jnp.where(row == 0, mine, other)
        out_ref[:, cols:] = jnp.where(row == 0, other, mine)

    arrays = [((tile, cols), tiled, part) for part in parts]
    out = ((2 * rows, 2 * cols), (tile, 2 * cols), lambda i, *_: (i + skip, 0))
    return assemble("in_grad", meta, arrays, tiles, out, fill, before)


def finish_qkv(meta, parts):
    feats, tile = parts[0][0].shape[1], 256
    blocks = [(2 * HS, tile), (HS, tile)] * 2

    def fill(read, row, out_ref):
        mine, other = (jnp.concatenate([read(k), read(k + 1)], 0).T for k in (0, 2))
        out_ref[:, 0, :] = jnp.where(row == 0, mine, other)
        out_ref[:, 1, :] = jnp.where(row == 0, other, mine)

    arrays = [(block, lambda i, *_: (0, i), part) for block, part in zip(blocks, parts, strict=True)]
    out = ((feats, 2, 3 * HS), (tile, 2, 3 * HS), lambda i, *_: (i, 0, 0))
    return assemble("qkv_grad", meta, arrays, feats // tile, out, fill)


def finish_dense(meta, parts):
    feats = parts[0][0].shape[1]

    def fill(read, row, out_ref):
        out_ref[row] = read(0)
        out_ref[1 - row] = read(1)

    arrays = [((HS, feats), lambda *_: (1, 0), part) for part in parts]
    out = ((2, HS, feats), (2, HS, feats), lambda *_: (0, 0, 0))
    return assemble("dense_grad", meta, arrays, 1, out, fill)


class Names:
    def __getattr__(self, name):
        return name


def is_name(value):
    return isinstance(value, (str, tuple))


class Beats:
    def __init__(self):
        self.env, self.tasks, self.flying = {}, [], []
        self.now, self.token = 0, jnp.zeros((8, LANES), F32)
        self.last, self.new = self.token, []
        self.line = Line()

    def compute(self, beat, names, fn, *inputs, top=False):
        self.tasks.append((beat, inputs, names, (fn, None) if top else fn))

    def send(self, beat, name, fn, source, beats=1):
        self.tasks.append((beat, (source,), name, (fn, beats)))

    def put(self, name, value):
        self.env[name] = value
        self.new.append(name)

    def run(self):
        while self.tasks or self.flying or self.line.busy:
            if self.now > 20 + 8 * self.line.count:
                raise ValueError([task[:3] for task in self.tasks])
            self.line.beat(self)
            for task in [t for t in self.tasks if isinstance(t[3], tuple)] + self.tasks[:]:
                beat, inputs, names, fn = task
                if not any(task is t for t in self.tasks):
                    continue
                if beat > self.now or any(is_name(i) and i not in self.env for i in inputs):
                    continue
                self.tasks = [t for t in self.tasks if t is not task]
                values = [self.env[i] if is_name(i) else i for i in inputs]
                if isinstance(fn, tuple) and fn[1] is None:
                    self.do(names, fn[0], *values)
                elif isinstance(fn, tuple):
                    fn, beats = fn
                    value = fn(tie(values[0], self.token))
                    if beats:
                        self.flying.append((self.now + beats, names, value))
                    else:
                        self.env[names] = value
                else:
                    self.do(names, fn, *values)
            self.tick()

    def do(self, names, fn, first, *rest):
        outs = fn(tie(first, self.last), *rest)
        for name, value in [(names, outs)] if is_name(names) else zip(names, outs, strict=True):
            self.put(name, value)
        self.last = jax.tree.leaves(outs)[0]
        return outs

    def tick(self):
        self.now += 1
        for due, name, value in self.flying:
            if due <= self.now:
                self.put(name, value)
        self.flying = [f for f in self.flying if f[0] > self.now]
        names = list(dict.fromkeys(n for n in self.new if n in self.env))
        values = lax.optimization_barrier((self.token, *[self.env[n] for n in names]))
        self.token = self.last = values[0]
        self.env.update(zip(names, values[1:], strict=True))
        self.new = []


class Line:
    def __init__(self):
        self.count, self.place = lax.axis_size("dp"), lax.axis_index("dp")
        self.mid = self.count // 2
        self.queue, self.going = [], []

    @property
    def busy(self):
        return bool(self.queue or self.going)

    def enter(self, *names):
        self.queue += names

    def on(self, *places):
        return (self.place == places[0]) | (self.place == places[1])

    def pairs(self, step):
        n, mid = self.count, self.mid
        if step < mid - 1:
            return [(step, step + 1), (n - 1 - step, n - 2 - step)]
        if step == mid - 1:
            return [(mid - 1, mid), (mid, mid - 1)]
        step -= mid
        return [(mid - 1 - step, mid - 2 - step), (mid + step, mid + 1 + step)]

    def beat(self, beats):
        env, mid, steps = beats.env, self.mid, 2 * self.mid - 1
        later, outward = [], {}
        for name, step in self.going:
            got, value = (name, step), (name, "held")
            if step + 1 == steps:
                src = self.pairs(step)
                held, arrived = env[value], env[got]
                env[name, "sum"] = jnp.where(self.on(src[0][1], src[1][1]), arrived, held)
                env[name, "parts"] = self.on(src[0][1], src[1][1]), arrived, held
            else:
                later.append((name, step + 1))
        starting = []
        if self.queue and self.queue[0] in env and self.queue[0] != "small":
            starting = [self.queue.pop(0)]
            env[starting[0], "held"] = env[starting[0]]
        small = [n for n in self.queue if n == "small" and n in env]
        for n in small:
            self.queue.remove(n)
            env[n, "held"] = env[n]
            starting.append(n)
        moving = [(n, 0) for n in starting] + later

        def update(name, step):
            if step == 0:
                return (lambda v: v), [(name, "held")]
            inputs = [(name, "held"), (name, step - 1)]
            if step <= mid:
                return add_low, inputs
            src = self.pairs(step - 1)
            return choose(self.on(src[0][1], src[1][1])), inputs

        for name, step in moving:
            match = [
                m
                for m in moving
                if step >= mid
                and m[1] == 2 * mid - 2 - step
                and env[m[0]].shape == env[name].shape
                and m not in outward
            ]
            if match:
                outward[match[0]] = (name, step)
        joint = self.add_jointly(beats, moving, outward)
        for name, step in sorted(moving, key=lambda m: (m[1] != mid - 1, m[1] < mid)):
            if (name, step) in outward or (name, step) in outward.values():
                continue
            if step and (name, step) not in joint:
                fn, inputs = update(name, step)
                beats.do((name, "held"), fn, *[env[i] for i in inputs])
            self.send(beats, self.pairs(step), (name, "held"), [(name, step)])
        for (name, step), (far, far_step) in outward.items():
            if (far, far_step) not in joint:
                fn, inputs = update(name, step)
                if step:
                    beats.do((name, "held"), fn, *[env[i] for i in inputs])
                inputs = update(far, far_step)[1]
                outer = self.on(step, self.count - 1 - step)
                if far_step > mid:
                    gets = self.on(*[pair[1] for pair in self.pairs(far_step - 1)])
                    beats.do((far, "held"), choose(gets), *[env[i] for i in inputs])
                    beats.do((far, "held"), choose(outer), env[far, "held"], env[name, "held"])
                else:
                    add = choose_or_add(outer)
                    beats.do((far, "held"), add, env[name, "held"], *[env[i] for i in inputs])
            self.send(
                beats,
                self.pairs(step) + self.pairs(far_step),
                (far, "held"),
                [(name, step), (far, far_step)],
            )
        self.going = moving

    def add_jointly(self, beats, moving, outward):
        env, mid = beats.env, self.mid
        for far, far_step in moving:
            shape = env[far].shape
            mine = [m for m, step in moving if step == mid - 1 and step and env[m].shape == shape]
            inner = [m for m, out in outward.items() if out == (far, far_step)]
            if far_step != mid or not mine or len(shape) != 2 or (inner and inner[0][1]):
                continue
            keys = [(mine[0], "held"), (far, "held")]
            arrays = [env[mine[0], "held"], env[mine[0], mid - 2], env[far, "held"], env[far, mid - 1]]
            outs, flag = [(shape[1], BF)] * 2, None
            if inner:
                arrays.append(env[inner[0][0], "held"])
                flag = self.on(0, self.count - 1)

            def add(*v):
                a, b, c, d = v[-5:-1] if inner else v
                both = plain_add(a, b) + plain_add(c, d)
                return both[:1] + [jnp.where(v[0], v[-1], both[1])] if inner else both

            beats.do(keys, lambda *v: rowwise(add, shape[0], outs, *v, flag=flag), *arrays)
            return [(mine[0], mid - 1), (far, far_step)]
        return []

    def send(self, beats, pairs, source, gets):
        value = lax.ppermute(tie(beats.env[source], beats.token), "dp", pairs)
        for name, step in gets:
            beats.flying.append((beats.now + 1, (name, step), value))


def per_device(
    residual_in,
    attn_gain,
    attn_shift,
    mlp_gain,
    mlp_shift,
    qkv_weight,
    qkv_bias,
    dense_weight,
    dense_bias,
    in_weight,
    in_bias,
    out_weight,
    out_bias,
    cotangent,
):
    row, col = lax.axis_index("row"), lax.axis_index("col")
    rows, feats = residual_in.shape
    slots, width = lax.axis_size("col"), 2 * feats
    units = in_weight.shape[1] // 2
    other = 1 - row
    plan = Beats()
    env, compute, send, n = plan.env, plan.compute, plan.send, Names()

    def summed(name):
        return name, n.sum


    def below(*parts):
        return jnp.concatenate(parts, 0)

    def part(lo, hi):
        return lambda v: lax.slice_in_dim(v, lo, hi)

    def share(beat, name, fn, source, *needs):
        compute_free = (beat, (source, *needs), name, (fn, 0))
        plan.tasks.append(compute_free)

    env.update(res=residual_in, cot=cotangent)
    env[n.gx] = jnp.stack([attn_gain, attn_shift, mlp_gain, mlp_shift])

    send(0, n.gy, swap_row, n.gx)
    send(0, n.res_x, swap_row, n.res)
    send(0, n.res_y, swap_y, n.res)
    send(0, n.res_c, swap_core, n.res)
    mid = feats // 2
    pick = lax.dynamic_slice
    compute(0, n.in_sent0, lambda w: pick(w, (0, other * units), (mid, units)), in_weight)
    compute(0, n.wx, lambda w: half(w, 1, row), in_weight)
    compute(0, n.ox, lambda w: half(w, 0, row), out_weight)
    compute(0, n.in_sent1, lambda w: pick(w, (mid, other * units), (mid, units)), in_weight)

    compute(0, [n.cos, n.low, n.high], lambda _: rotary_tables(slots * rows), n.gx)

    send(1, n.wy0, swap_row, n.in_sent0)
    send(1, n.res_xy, swap_y, n.res_x)
    send(1, n.res_xc, swap_core, n.res_x)
    send(1, n.res_yc, swap_core, n.res_y)
    compute(1, n.norm0, lambda *a: norm_call(col, 0, *a), n.res, n.res_x, n.gx, n.gy)
    for i in range(2):
        at = other * units + i * (units // 2)
        compute(1, (n.oy_sent, i), lambda w, at=at: pick(w, (at, 0), (units // 2, feats)), out_weight)
    compute(1, n.qx, lambda w: lax.dynamic_index_in_dim(w, row, 1, False), qkv_weight)
    compute(1, n.dense_sent, lambda w: lax.dynamic_index_in_dim(w, other, 0, False), dense_weight)
    compute(1, n.dx, lambda w: lax.dynamic_index_in_dim(w, row, 0, False), dense_weight)

    send(2, n.wy1, swap_row, n.in_sent1)
    send(2, n.res_xyc, swap_core, n.res_xy, 0)

    def gather_col(value):
        return lax.all_gather(value, "col", axis=0, tiled=True)

    share(2, n.g, gather_col, n.cot)

    def norm_rest(res_c, res_xc, res_y, res_xy, res_yc, res_xyc, gx, gy, before):
        before = norm_call(col, 1, res_c, res_xc, gx, gy, *before)
        before = norm_call(col, 2, res_y, res_xy, gx, gy, *before)
        return norm_call(col, 3, res_yc, res_xyc, gx, gy, *before)

    compute(
        2,
        [n.ax, n.ay, n.mx, n.my],
        norm_rest,
        *[n.res_c, n.res_xc, n.res_y, n.res_xy, n.res_yc, n.res_xyc, n.gx, n.gy, n.norm0],
    )

    send(3, n.cot_x, swap_row, n.cot)
    in_bias_mine = lax.dynamic_slice_in_dim(in_bias, row * units, units, 0)
    compute(3, [n.active, n.slope], pre_call, n.mx, n.my, n.wx, n.wy0, n.wy1, in_bias_mine)

    def grads(beat, names, cuts, *inputs, **keys):
        compute(beat, names, lambda *a: weight_grad(cuts, *a, **keys), *inputs)

    two = [units // 2] * 2
    half_units = [units // 2]
    grads(3, [n.out_own0], half_units, n.active, n.g, vmem=58)
    z = 4
    for i in range(2):
        send(z + i, (n.oy, i), swap_row, (n.oy_sent, i))
    oy = [(n.oy, 0), (n.oy, 1)]
    compute(z, [n.out_own1], lambda a, g: weight_grad(half_units, (a, units // 2), g, vmem=58), n.active, n.g)
    share(z, n.h, gather_col, n.cot_x)
    compute(z, n.x_near, below, n.res, n.res_y)
    compute(z, n.y_near, below, n.res_x, n.res_xy)
    compute(z, n.x_far, below, n.res_c, n.res_yc)
    compute(z, n.y_far, below, n.res_xc, n.res_xyc)
    grads(z + 1, [n.out_oth0, n.out_oth1], two, n.active, n.h, vmem=58)
    compute(z + 2, [n.pre_grad, n.in_bias_sum], pre_grad_call, n.g, n.h, n.ox, *oy, n.slope)
    two = [feats // 2] * 2
    grads(z + 3, [n.in_own0, n.in_own1], two, n.mx, n.pre_grad)
    grads(z + 3, [n.in_oth0, n.in_oth1], two, n.my, n.pre_grad)
    cut = 5 * feats // 8
    for i, (lo, hi) in enumerate(((0, cut), (cut, feats))):
        sent = (n.qy_sent, i)
        compute(2, sent, lambda w, lo=lo, hi=hi: lax.dynamic_index_in_dim(w[lo:hi], other, 1, False), qkv_weight)
        send(z + 2 + i, (n.qy, i), swap_row, sent)
    send(z + 3, n.dy, swap_row, n.dense_sent)
    compute(z + 4, n.qy, below, (n.qy, 0), (n.qy, 1))
    qkv_bias_mine = lax.dynamic_index_in_dim(qkv_bias, row, 0, False)
    compute(
        z + 4,
        [n.query, n.key, n.value],
        packed_call,
        *[n.ax, n.ay, n.qx, n.qy, qkv_bias_mine, n.cos, n.low, n.high],
    )
    compute(
        z + 4,
        n.attended_grad,
        lambda g, h, dx, dy: (dot(g, dx, NT) + dot(h, dy, NT)).astype(BF),
        *[n.g, n.h, n.dx, n.dy],
    )
    compute(
        z + 5,
        [n.packed_grad, n.attended, n.qkv_bias_sum],
        lambda *a: attention(slots, *a),
        *[n.query, n.key, n.value, n.attended_grad, n.cos, n.low, n.high],
    )
    cuts = [2 * HS, 2 * HS]
    grads(z + 6, [n.att_own0, n.att_own1], cuts, n.packed_grad, n.ax, n.attended, n.g)
    grads(z + 6, [n.att_oth0, n.att_oth1], cuts, n.packed_grad, n.ay, n.attended, n.h)

    send(z + 4, n.in_oth0_x, swap_row, n.in_oth0)
    send(z + 5, n.in_oth1_x, swap_row, n.in_oth1)
    send(z + 7, n.att_oth0_x, swap_row, n.att_oth0)
    send(z + 8, n.att_oth1_x, swap_row, n.att_oth1)
    plan.line.enter(
        *(n.out_own0, n.out_own1, n.out_oth0, n.out_oth1, n.in_own0, n.in_own1, n.in_oth0_x),
        *(n.att_own0, n.att_own1, n.att_oth0_x, n.att_oth1_x, n.in_oth1_x, n.small),
    )

    def choose_part(parts):
        return choose(parts[0])(parts[2], parts[1])

    compute(z + 5, n.out_oth0_s, choose_part, (n.out_oth0, n.parts))
    compute(z + 6, n.out_oth1_s, choose_part, (n.out_oth1, n.parts))
    send(z + 6, n.out_oth0_y, swap_row, n.out_oth0_s)
    send(z + 9, n.out_oth1_y, swap_row, n.out_oth1_s)

    for beat, part, name, sums, x, y in (
        (z + 7, 1, (n.ng, n.far), n.sums_far, n.x_far, n.y_far),
        (z + 8, 0, (n.ng, n.near), n.sums_near, n.x_near, n.y_near),
    ):
        compute(
            beat,
            [name, sums],
            lambda *a, part=part: norm_grad_call(col, part, *a),
            *[x, y, n.gx, n.gy, n.packed_grad, n.pre_grad, n.qx, n.qy, n.wx, n.wy0, n.wy1],
        )
    for beat, part, name in ((z + 9, 1, (n.mixed, n.far)), (z + 10, 0, (n.mixed, n.near))):
        compute(
            beat,
            name,
            lambda *a, part=part: mixed_call(col, part, *a),
            *[n.attended, n.active, n.dx, n.dy, n.ox, *oy],
        )

    part_rows = rows // 2

    def near_sum(a, b, c):
        out = a.astype(F32) + b.astype(F32) + c.astype(F32)
        return [out[:, feats:].astype(BF), out[:, :feats]]

    outs = [(feats, BF), (feats, F32)]

    def near_part(i, join=False):
        at = i * part_rows

        def fn(a, b, c, *before):
            keys = dict(whole=rows, skip=at, before=before) if join else {}
            return rowwise(near_sum, part_rows, outs, (a, at), (b, at), c, vmem=58, **keys)

        return fn

    def far_sum(i):
        at, outs = rows + i * part_rows, [(width, BF)]
        return lambda a, b: rowwise(plain_add, part_rows, outs, (a, at), (b, at), vmem=58)[0]

    def scatter(beat, name, last=False):
        far, mine, got = [(name, i) for i in (n.far, n.near, n.core)]
        send(beat, got, swap_core, far, 0)
        got_y = [(name, n.near, i) for i in range(2)]
        for i in range(2):
            far_y = (name, n.far, i)
            compute(beat + i, far_y, far_sum(i), mine, got)
            send(beat + 1 + i, got_y[i], swap_y, far_y)
        if last:
            for i in range(2):
                sent = (name, n.sent, i)
                compute(beat + 3, [sent, (name, n.keep, i)], near_part(i), mine, got, got_y[i], top=True)
                send(beat + 3, (name, n.got, i), swap_row, sent)
            return
        half_sent, half_keep = [(name, part, 0) for part in (n.sent, n.keep)]
        compute(beat + 2, [half_sent, half_keep], near_part(0, True), mine, got, got_y[0])
        last_part = [near_part(1, True), mine, got, got_y[1], half_sent, half_keep]
        compute(beat + 3, [(name, n.sent), (name, n.keep)], *last_part, top=True)
        send(beat + 3, (name, n.got), swap_row, (name, n.sent))

    scatter(z + 8, n.ng)
    scatter(z + 10, n.mixed, last=True)
    compute(
        z + 14,
        n.block_out,
        lambda a0, a1, x0, x1, res, b, c: (
            res.astype(F32) + below(a0, a1) + below(x0, x1).astype(F32) + b + c
        ).astype(BF),
        *[(n.mixed, part, i) for part in (n.keep, n.got) for i in range(2)],
        *[n.res, dense_bias, out_bias],
    )

    def own_norm(res, res_x):
        x, y = res.astype(F32), res_x.astype(F32)
        average = (jnp.sum(x, 1, keepdims=True) + jnp.sum(y, 1, keepdims=True)) / width
        squares = (jnp.sum(x * x, 1, keepdims=True) + jnp.sum(y * y, 1, keepdims=True)) / width
        scale = lax.rsqrt(squares - average * average + EPSILON)
        return (x - average) * scale, scale

    def token_sums(keep, xg, res, res_x):
        normed, scale = own_norm(res, res_x)
        grad = keep + xg.astype(F32)
        return jnp.stack([jnp.sum(grad, 1), jnp.sum(grad * normed, 1)])

    compute(z + 12, n.tok, token_sums, (n.ng, n.keep), (n.ng, n.got), n.res, n.res_x)
    send(z + 12, n.tok_x, swap_row, n.tok, 0)

    def finish_input(keep, xg, res, res_x, cot, tok, tok_x):
        normed, scale = own_norm(res, res_x)
        tok = (tok + tok_x) / width
        grad = keep + xg.astype(F32)
        return cot.astype(F32) + scale * (grad - tok[0][:, None] - normed * tok[1][:, None])

    rest = [n.res, n.res_x, n.cot, n.tok, n.tok_x]
    compute(
        z + 12, n.input_grad, finish_input, (n.ng, n.keep), (n.ng, n.got), *rest
    )

    def small_all(near, far, cot, qkv_bias_sum, in_bias_sum):
        bias_sum = jnp.pad(jnp.sum(cot, 0, dtype=F32), (0, feats))
        parts = [(near + far).reshape(-1), bias_sum, qkv_bias_sum.reshape(-1), in_bias_sum.reshape(-1)]
        return jnp.concatenate(parts)

    def take(parts):
        return jnp.where(parts[0], parts[1], parts[2])

    compute(z + 8, n.small, small_all, n.sums_near, n.sums_far, n.cot, n.qkv_bias_sum, n.in_bias_sum)
    compute(z + 12, n.small_s, take, (n.small, n.parts), top=True)
    send(z + 12, n.small_x, swap_row, n.small_s)

    def by_feature(mine, got):
        mine, got = (v[: 5 * width].reshape(5, width) for v in (mine, got))
        return mine[:, :feats] + got[:, feats:]

    compute(z + 13, n.small0, by_feature, n.small_s, n.small_x)
    send(z + 13, n.small0_c, swap_core, n.small0, 0)
    compute(z + 13, n.small1, jnp.add, n.small0, n.small0_c)
    send(z + 13, n.small1_y, swap_y, n.small1, 0)
    compute(z + 13, n.small2, jnp.add, n.small1, n.small1_y)

    def finish(beat, name, fn, *sources):
        def step(*sources):
            flag = next(v[0] for v in sources if isinstance(v, tuple))
            arrays = [v[1:] if isinstance(v, tuple) else (v,) for v in sources]
            return fn(jnp.stack([row, flag.astype(jnp.int32)]), arrays)

        compute(beat, name, step, *sources)

    def done(*names):
        return [(v, n.parts) for v in names]

    finish(z + 12, n.out_weight_grad, finish_out, *done(n.out_own0, n.out_own1), n.out_oth0_y, n.out_oth1_y)
    att = done(n.att_own0, n.att_own1, n.att_oth0_x, n.att_oth1_x)
    finish(z + 13, n.qkv_weight_grad, finish_qkv, *att)
    finish(z + 13, n.dense_weight_grad, finish_dense, att[1], att[3])
    finish(z + 11, n.in_grad0, finish_in, *done(n.in_own0, n.in_oth0_x))

    def second(meta, arrays):
        return finish_in(meta, arrays[:2], arrays[2][0])

    finish(z + 14, n.in_weight_grad, second, *done(n.in_own1, n.in_oth1_x), n.in_grad0)
    plan.run()
    def in_order(mine, got):
        return jnp.where(row == 0, jnp.concatenate([mine, got]), jnp.concatenate([got, mine]))

    by_feature = env[n.small2]
    by_col, by_col_got = (env[name][5 * width :] for name in (n.small_s, n.small_x))
    qkv_bias_grad = in_order(by_col[: 3 * HS], by_col_got[: 3 * HS]).reshape(2, 3 * HS)
    in_bias_grad = in_order(by_col[3 * HS :], by_col_got[3 * HS :])
    return (
        env[n.block_out],
        env[n.input_grad],
        by_feature[0],
        by_feature[1],
        by_feature[2],
        by_feature[3],
        env[n.qkv_weight_grad],
        qkv_bias_grad,
        env[n.dense_weight_grad],
        by_feature[4],
        env[n.in_weight_grad],
        in_bias_grad,
        env[n.out_weight_grad],
        by_feature[4],
    )


def solution(mesh):
    in_specs = (
        P(("dp", "col"), "row"),
        P("row"),
        P("row"),
        P("row"),
        P("row"),
        P("row", "col", None),
        P("col", None),
        P("col", None, "row"),
        P("row"),
        P("row", "col"),
        P("col"),
        P("col", "row"),
        P("row"),
        P(("dp", "col"), "row"),
    )
    out_specs = (
        P(("dp", "col"), "row"),
        P(("dp", "col"), "row"),
        P("row"),
        P("row"),
        P("row"),
        P("row"),
        P("row", "col", None),
        P("col", None),
        P("col", None, "row"),
        P("row"),
        P("row", "col"),
        P("col"),
        P("col", "row"),
        P("row"),
    )
    return jax.shard_map(
        per_device, mesh=mesh, in_specs=in_specs, out_specs=out_specs, check_vma=False
    )
```

```python
import math

import jax
import jax.numpy as jnp
from jax import lax
from jax.experimental import pallas as pl
from jax.experimental.pallas import tpu as pltpu
from jax.sharding import PartitionSpec as P

HS = 256
ROT = 64
LENGTH = 2048
LANES = 128
EPSILON = 1e-05
ROPE_BASE = 10000.0
NEGATIVE = -1e30
BF = jnp.bfloat16
F32 = jnp.float32
NN, NT, TN = ((1,), (0,)), ((1,), (1,)), ((0,), (0,))
MIB = 2**20
COST = pl.CostEstimate(flops=0, bytes_accessed=0, transcendentals=0)


def tie(value, *others):
    return lax.optimization_barrier((value,) + others)[0]


def swap_row(value):
    return lax.ppermute(value, "row", [(0, 1), (1, 0)])


def swap_col(value, bit):
    return lax.ppermute(value, "col", [(i, i ^ bit) for i in range(lax.axis_size("col"))])


def swap_y(value):
    return swap_col(value, 2)


def swap_core(value):
    return swap_col(value, 1)


def half(array, axis, index):
    size = array.shape[axis] // 2
    return lax.dynamic_slice_in_dim(array, index * size, size, axis)


def dot(a, b, dims):
    return lax.dot_general(a, b, (dims, ((), ())), preferred_element_type=F32)


def rotary_tables(tokens):
    position = (jnp.arange(tokens) % LENGTH).astype(F32)
    lane = jnp.arange(LANES)
    index = (lane % (ROT // 2)).astype(F32)
    frequency = ROPE_BASE ** (-(2.0 * index) / ROT)
    angle = position[:, None] * frequency[None, :]
    cos = jnp.where(lane < ROT, jnp.cos(angle), 1.0)
    sin = jnp.sin(angle)
    low = jnp.where(lane < ROT // 2, -sin, 0.0)
    high = jnp.where((lane >= ROT // 2) & (lane < ROT), sin, 0.0)
    return cos, low, high


def rotate(values, cos, low, high):
    first = values[:, :LANES]
    up = pltpu.roll(first, LANES - ROT // 2, 1)
    down = pltpu.roll(first, ROT // 2, 1)
    first = first * cos + up * low + down * high
    return jnp.concatenate([first, values[:, LANES:]], 1)


def tiled(i, *_):
    return (i, 0)


def fixed(*_):
    return (0, 0)


def call(kernel, name, steps, ins, outs, col=None, vmem=28, tile=None):
    def block(shape, index, rows=None):
        rows = rows or (shape[0] if index is fixed else tile or shape[0] // steps)
        return pl.BlockSpec((rows, shape[1]), index)

    spec = pltpu.PrefetchScalarGridSpec(
        num_scalar_prefetch=0 if col is None else 1,
        grid=(steps,),
        in_specs=[block(a.shape, index) for a, index in ins],
        out_specs=tuple(block(shape, index, rows) for shape, _, rows, index in outs),
    )
    return pl.pallas_call(
        kernel if col is None else lambda _, *refs: kernel(*refs),
        grid_spec=spec,
        out_shape=tuple(jax.ShapeDtypeStruct(shape, dtype) for shape, dtype, _, _ in outs),
        compiler_params=pltpu.CompilerParams(vmem_limit_bytes=vmem * MIB),
        cost_estimate=COST,
        name=name,
    )(*([] if col is None else [col.reshape(1)]), *[a for a, _ in ins])


def normed_halves(x_ref, y_ref):
    x, y = x_ref[...].astype(F32), y_ref[...].astype(F32)
    width = x.shape[1] + y.shape[1]
    average = (jnp.sum(x, 1, keepdims=True) + jnp.sum(y, 1, keepdims=True)) / width
    squares = (jnp.sum(x * x, 1, keepdims=True) + jnp.sum(y * y, 1, keepdims=True)) / width
    scale = lax.rsqrt(squares - average * average + EPSILON)
    return (x - average) * scale, (y - average) * scale


def norm_kernel(x_ref, y_ref, gx_ref, gy_ref, ax_ref, ay_ref, mx_ref, my_ref):
    x, y = normed_halves(x_ref, y_ref)
    ax_ref[...] = (x * gx_ref[0:1] + gx_ref[1:2]).astype(BF)
    ay_ref[...] = (y * gy_ref[0:1] + gy_ref[1:2]).astype(BF)
    mx_ref[...] = (x * gx_ref[2:3] + gx_ref[3:4]).astype(BF)
    my_ref[...] = (y * gy_ref[2:3] + gy_ref[3:4]).astype(BF)


def norm_call(col, flip, x, y, gx, gy, *before):
    (rows, feats), tile, slots = x.shape, 256, 4
    steps = rows // tile

    def index(i, col_ref):
        return ((col_ref[0] ^ flip) * steps + i, 0)

    rest = [pl.BlockSpec(memory_space=pl.ANY)] * len(before)
    block = pl.BlockSpec((tile, feats), tiled)
    whole = pl.BlockSpec(gx.shape, fixed)
    return pl.pallas_call(
        lambda _, x, y, gx, gy, *refs: norm_kernel(x, y, gx, gy, *refs[len(before) :]),
        grid_spec=pltpu.PrefetchScalarGridSpec(
            num_scalar_prefetch=1,
            grid=(steps,),
            in_specs=[block, block, whole, whole] + rest,
            out_specs=(pl.BlockSpec((tile, feats), index),) * 4,
        ),
        out_shape=(jax.ShapeDtypeStruct((slots * rows, feats), BF),) * 4,
        input_output_aliases={5 + i: i for i in range(len(before))},
        compiler_params=pltpu.CompilerParams(vmem_limit_bytes=58 * MIB),
        cost_estimate=COST,
        name="norm",
    )(col.reshape(1), x, y, gx, gy, *before)


def pre_kernel(x_ref, y_ref, wx_ref, wy0_ref, wy1_ref, bias_ref, active_ref, slope_ref):
    mid, part = wy0_ref.shape[0], wx_ref.shape[1]
    for start in range(0, wx_ref.shape[1], part):
        at = slice(start, start + part)
        u = dot(x_ref[...], wx_ref[:, at], NN) + bias_ref[:, at]
        u = u + dot(y_ref[:, :mid], wy0_ref[:, at], NN) + dot(y_ref[:, mid:], wy1_ref[:, at], NN)
        phi = 0.5 * (1.0 + lax.erf(u * 2.0**-0.5))
        bell = jnp.exp(-0.5 * u * u)
        active_ref[:, at] = (u * phi).astype(BF)
        slope_ref[:, at] = (phi + u * bell * (2.0 * math.pi) ** (-0.5)).astype(BF)


def pre_call(x, y, wx, wy0, wy1, bias):
    tokens, tile, units = x.shape[0], 256, wx.shape[1]
    return call(
        pre_kernel,
        "pre_act",
        tokens // tile,
        [(x, tiled), (y, tiled), (wx, fixed), (wy0, fixed), (wy1, fixed), (bias.reshape(1, -1), fixed)],
        [((tokens, units), BF, tile, tiled)] * 2,
        vmem=58,
    )


def rowwise(fn, rows, outs, *ins, flag=None, vmem=20, whole=None, skip=0, before=()):
    tile = 256
    ins = [i if isinstance(i, tuple) else (i, 0) for i in ins]
    flags = [] if flag is None else [flag.astype(jnp.int32).reshape(1)]

    def at(first):
        return fixed if first is None else lambda i, *_: (i + first // tile, 0)

    def kernel(*refs):
        values = [ref[0] != 0 for ref in refs[: len(flags)]]
        refs = refs[len(flags) :]
        results = fn(*values, *[ref[...] for ref in refs[: len(ins)]])
        for ref, result in zip(refs[len(ins) + len(before) :], results, strict=True):
            ref[...] = result

    first_in = len(flags) + len(ins)
    return pl.pallas_call(
        kernel,
        grid_spec=pltpu.PrefetchScalarGridSpec(
            num_scalar_prefetch=len(flags),
            grid=(rows // tile,),
            in_specs=[pl.BlockSpec((tile, a.shape[1]), at(first)) for a, first in ins]
            + [pl.BlockSpec(memory_space=pl.ANY)] * len(before),
            out_specs=tuple(pl.BlockSpec((tile, cols), at(skip)) for cols, _ in outs),
        ),
        out_shape=tuple(jax.ShapeDtypeStruct((whole or rows, cols), dtype) for cols, dtype in outs),
        input_output_aliases={first_in + i: i for i in range(len(before))},
        compiler_params=pltpu.CompilerParams(vmem_limit_bytes=vmem * MIB),
        cost_estimate=COST,
        name="rowwise",
    )(*flags, *[a for a, _ in ins], *before)


def plain_add(a, b):
    return [(a.astype(F32) + b.astype(F32)).astype(BF)]


def add_low(a, b):
    return (a.astype(F32) + b.astype(F32)).astype(a.dtype)


def choose(flag):
    def fn(held, arrived):
        if held.ndim == 1:
            return jnp.where(flag, arrived, held)
        outs = [(held.shape[1], BF)]
        return rowwise(lambda f, h, a: [jnp.where(f, a, h)], held.shape[0], outs, held, arrived, flag=flag)[0]

    return fn


def choose_or_add(flag):
    return lambda value, a, b: jnp.where(flag, value, add_low(a, b))


def weight_grad(cuts, a, b, last_a=None, last_b=None, vmem=20):
    tokens, cols, tile = b.shape[0], b.shape[1], 256
    own = sum(cuts) // tile if last_a is None else a.shape[1] // tile
    skip = 0
    if isinstance(a, tuple):
        a, skip = a[0], a[1] // tile
    first = [sum(cuts[:i]) // tile for i in range(len(cuts) + 1)]

    def kernel(*refs):
        step = pl.program_id(0)

        def store(out):
            for start, end, ref in zip(first[:-1], first[1:], refs[-len(cuts) :], strict=True):

                @pl.when((step >= start) & (step < end))
                def _():
                    ref[...] = out

        if last_a is None:
            store(dot(refs[0][...], refs[1][...], TN).astype(BF))
            return

        @pl.when(step < own)
        def _():
            store(dot(refs[0][...], refs[1][...], TN).astype(BF))

        @pl.when(step >= own)
        def _():
            store(dot(refs[2][...], refs[3][...], TN).astype(BF))

    def index(start, end):
        return lambda i: (jnp.clip(i - start, 0, end - start - 1), 0)

    ins = [a, b] if last_a is None else [a, b, last_a, last_b]
    specs = [
        pl.BlockSpec((tokens, tile), lambda i: (0, jnp.minimum(i, own - 1) + skip)),
        pl.BlockSpec(b.shape, fixed),
        pl.BlockSpec((tokens, tile), fixed),
        pl.BlockSpec(b.shape, fixed),
    ]
    return pl.pallas_call(
        kernel,
        grid=(first[-1],),
        out_shape=tuple(jax.ShapeDtypeStruct((size, cols), BF) for size in cuts),
        in_specs=specs[: len(ins)],
        out_specs=tuple(
            pl.BlockSpec((tile, cols), index(s, e)) for s, e in zip(first[:-1], first[1:], strict=True)
        ),
        compiler_params=pltpu.CompilerParams(vmem_limit_bytes=vmem * MIB),
        cost_estimate=COST,
        name="weight_grad",
    )(*ins)


def pre_grad_kernel(gx_ref, gy_ref, wx_ref, wy0_ref, wy1_ref, slope_ref, out_ref, sum_ref):
    @pl.when(pl.program_id(0) == 0)
    def _():
        sum_ref[...] = jnp.zeros_like(sum_ref)

    mid = wy0_ref.shape[0]
    for i, wy_ref in enumerate((wy0_ref, wy1_ref)):
        at = slice(i * mid, (i + 1) * mid)
        u = dot(gx_ref[...], wx_ref[at, :], NT) + dot(gy_ref[...], wy_ref[...], NT)
        low = (u * slope_ref[:, at].astype(F32)).astype(BF)
        out_ref[:, at] = low
        sum_ref[:, at] += jnp.sum(low.astype(F32), 0, keepdims=True)


def pre_grad_call(gx, gy, wx, wy0, wy1, slope):
    tokens, tile, units = gx.shape[0], 512, wx.shape[0]
    return call(
        pre_grad_kernel,
        "pre_grad",
        tokens // tile,
        [(gx, tiled), (gy, tiled), (wx, fixed), (wy0, fixed), (wy1, fixed), (slope, tiled)],
        [((tokens, units), BF, tile, tiled), ((1, units), F32, 1, fixed)],
    )


def packed_kernel(x_ref, y_ref, wx_ref, wy_ref, bias_ref, cos_ref, low_ref, high_ref, q_ref, k_ref, v_ref):
    out = dot(x_ref[...], wx_ref[...], NN) + dot(y_ref[...], wy_ref[...], NN) + bias_ref[...]
    tables = cos_ref[...], low_ref[...], high_ref[...]
    q_ref[...] = rotate(out[:, :HS], *tables).astype(BF)
    k_ref[...] = rotate(out[:, HS : 2 * HS], *tables).astype(BF)
    v_ref[...] = out[:, 2 * HS :].astype(BF)


def packed_call(x, y, wx, wy, bias, *tables):
    tokens, tile = x.shape[0], 512
    return call(
        packed_kernel,
        "packed",
        tokens // tile,
        [(x, tiled), (y, tiled), (wx, fixed), (wy, fixed), (bias.reshape(1, -1), fixed)]
        + [(t, tiled) for t in tables],
        [((tokens, HS), BF, tile, tiled)] * 3,
    )


def attention_kernel(
    q_ref, k_ref, v_ref, g_ref, cos_ref, low_ref, high_ref, o_ref, out_ref, sum_ref, dk_acc, dv_acc
):
    slots, rows, _ = q_ref.shape
    scale = HS ** (-0.5)
    mask = lax.broadcasted_iota(jnp.int32, (rows, rows), 1) <= lax.broadcasted_iota(
        jnp.int32, (rows, rows), 0
    )
    total_sum = [jnp.zeros((1, HS), F32) for _ in range(3)]

    def unrotate(values, at):
        return rotate(values, cos_ref[at], -low_ref[at], -high_ref[at]).astype(BF)

    for i in range(slots):
        q, g = q_ref[i], g_ref[i]
        scores = []
        for j in range(i + 1):
            s = dot(q, k_ref[j], NT) * scale
            scores.append(jnp.where(mask, s, NEGATIVE) if j == i else s)
        top = scores[0].max(-1, keepdims=True)
        for s in scores[1:]:
            top = jnp.maximum(top, s.max(-1, keepdims=True))
        exps = [jnp.exp(s - top) for s in scores]
        inv = 1.0 / sum(e.sum(-1, keepdims=True) for e in exps)
        probs = [e * inv for e in exps]
        out = jnp.zeros((rows, HS), F32)
        center = jnp.zeros((rows, 1), F32)
        prob_grads = []
        for j in range(i + 1):
            low = probs[j].astype(BF)
            v = v_ref[j]
            out = out + dot(low, v, NN)
            pg = dot(g, v, NT)
            center = center + (probs[j] * pg).sum(-1, keepdims=True)
            prob_grads.append(pg)
            dv = dot(low, g, TN)
            if j == i:
                dv_acc[j] = dv
            else:
                dv_acc[j] += dv
        o_ref[i] = out.astype(BF)
        dq = jnp.zeros((rows, HS), F32)
        for j in range(i + 1):
            sg = (probs[j] * (prob_grads[j] - center)).astype(BF)
            dq = dq + dot(sg, k_ref[j], NN)
            dk = dot(sg, q, TN)
            if j == i:
                dk_acc[j] = dk
            else:
                dk_acc[j] += dk
        dq = unrotate(dq * scale, i)
        out_ref[i, :, 0:HS] = dq
        total_sum[0] = total_sum[0] + jnp.sum(dq.astype(F32), 0, keepdims=True)
    for j in range(slots):
        dk = unrotate(dk_acc[j] * scale, j)
        dv = dv_acc[j].astype(BF)
        out_ref[j, :, HS : 2 * HS] = dk
        out_ref[j, :, 2 * HS :] = dv
        total_sum[1] = total_sum[1] + jnp.sum(dk.astype(F32), 0, keepdims=True)
        total_sum[2] = total_sum[2] + jnp.sum(dv.astype(F32), 0, keepdims=True)
    for i in range(3):
        sum_ref[:, i * HS : (i + 1) * HS] = total_sum[i]


def attention(slots, q, k, v, g, cos, low, high):
    tokens = q.shape[0]
    rows = tokens // slots
    vmem = pl.BlockSpec(memory_space=pltpu.VMEM)
    attended, packed_grad, sums = pl.pallas_call(
        attention_kernel,
        out_shape=(
            jax.ShapeDtypeStruct((slots, rows, HS), BF),
            jax.ShapeDtypeStruct((slots, rows, 3 * HS), BF),
            jax.ShapeDtypeStruct((1, 3 * HS), F32),
        ),
        in_specs=[vmem] * 7,
        out_specs=(vmem,) * 3,
        scratch_shapes=[pltpu.VMEM((slots, rows, HS), F32)] * 2,
        compiler_params=pltpu.CompilerParams(vmem_limit_bytes=48 * MIB),
        cost_estimate=COST,
        name="attention",
    )(*[a.reshape(slots, rows, a.shape[1]) for a in (q, k, v, g, cos, low, high)])
    return packed_grad.reshape(tokens, 3 * HS), attended.reshape(tokens, HS), sums


def mixed_kernel(a_ref, b_ref, dx_ref, dy_ref, wx_ref, wy0_ref, wy1_ref, out_ref):
    feats, mid = dx_ref.shape[1], wy0_ref.shape[0]
    a, b = a_ref[...], b_ref[...]
    out_ref[:, :feats] = (dot(a, dx_ref[...], NN) + dot(b, wx_ref[...], NN)).astype(BF)
    y = dot(a, dy_ref[...], NN) + dot(b[:, :mid], wy0_ref[...], NN) + dot(b[:, mid:], wy1_ref[...], NN)
    out_ref[:, feats:] = y.astype(BF)


def mixed_call(col, part, attended, active, dx, dy, *weights):
    tokens, tile, width = attended.shape[0] // 2, 256, dx.shape[1] + dy.shape[1]
    steps = tokens // tile
    each = steps // 2

    def order(i, col_ref):
        return ((col_ref[0] ^ part ^ (2 * (i // each))) * each + i % each, 0)

    ins = [(attended, order), (active, order)] + [(w, fixed) for w in (dx, dy, *weights)]
    outs = [((tokens, width), BF, tile, tiled)]
    return call(mixed_kernel, "mixed", steps, ins, outs, col, tile=tile)[0]


def norm_grad_kernel(
    x_ref, y_ref, gx_ref, gy_ref, p_ref, u_ref, qx_ref, qy_ref, wx_ref, wy0_ref, wy1_ref, out_ref, sum_ref
):
    feats, mid = x_ref.shape[1], wy0_ref.shape[0]

    @pl.when(pl.program_id(0) == 0)
    def _():
        sum_ref[...] = jnp.zeros_like(sum_ref)

    normed = normed_halves(x_ref, y_ref)
    p, u = p_ref[...], u_ref[...]
    for start in range(0, 2 * feats, mid):
        side, lo = divmod(start, feats)
        at, part = slice(start, start + mid), slice(lo, lo + mid)
        q = (qx_ref, qy_ref)[side][part, :]
        w = wx_ref[part, :] if side == 0 else (wy0_ref, wy1_ref)[lo // mid][...]
        gains = (gx_ref, gy_ref)[side][:, part]
        n = normed[side][:, part]
        a, m = dot(p, q, NT), dot(u, w, NT)
        out_ref[:, at] = (a * gains[0:1] + m * gains[2:3]).astype(BF)
        sum_ref[0:1, at] += jnp.sum(a * n, 0, keepdims=True)
        sum_ref[1:2, at] += jnp.sum(a, 0, keepdims=True)
        sum_ref[2:3, at] += jnp.sum(m * n, 0, keepdims=True)
        sum_ref[3:4, at] += jnp.sum(m, 0, keepdims=True)


def norm_grad_call(col, part, x, y, gx, gy, packed_grad, pre_grad, *weights):
    tokens, tile, width = x.shape[0], 256, x.shape[1] + y.shape[1]
    steps = tokens // tile
    each = steps // 2

    def order(i, col_ref):
        return ((col_ref[0] ^ part ^ (2 * (i // each))) * each + i % each, 0)

    ins = [(x, tiled), (y, tiled), (gx, fixed), (gy, fixed), (packed_grad, order), (pre_grad, order)]
    return call(
        norm_grad_kernel,
        "norm_grad",
        steps,
        ins + [(w, fixed) for w in weights],
        [((tokens, width), BF, tile, tiled), ((4, width), F32, 4, fixed)],
        col,
        vmem=58,
        tile=tile,
    )


def assemble(name, meta, arrays, steps, out, fill, before=None):
    flat = [a for _, _, part in arrays for a in part]
    rest = [] if before is None else [before]
    shape, block, index = out

    def kernel(meta_ref, *refs):
        at = iter(refs[:-1])
        parts = [[next(at) for _ in part] for _, _, part in arrays]

        def read(i):
            values = [ref[...] for ref in parts[i]]
            value = values[0] if len(values) == 1 else jnp.where(meta_ref[1] != 0, *values)
            return value.astype(F32)

        fill(read, meta_ref[0], refs[-1])

    return pl.pallas_call(
        kernel,
        grid_spec=pltpu.PrefetchScalarGridSpec(
            num_scalar_prefetch=1,
            grid=(steps,),
            in_specs=[pl.BlockSpec(block, index) for block, index, part in arrays for _ in part]
            + [pl.BlockSpec(memory_space=pl.ANY)] * len(rest),
            out_specs=pl.BlockSpec(block, index),
        ),
        out_shape=jax.ShapeDtypeStruct(shape, F32),
        input_output_aliases={1 + len(flat): 0} if rest else {},
        compiler_params=pltpu.CompilerParams(vmem_limit_bytes=58 * MIB),
        cost_estimate=COST,
        name=name,
    )(meta, *flat, *rest)


def rows_of(part, tiles):
    return lambda i, *_: (jnp.clip(i - part * tiles, 0, tiles - 1), 0)


def finish_out(meta, parts):
    rows, cols = parts[0][0].shape
    tile, tiles = 256, rows // 256
    block = (tile, cols)

    def index(i, meta_ref):
        return ((i // (2 * tiles) ^ meta_ref[0]) * 2 * tiles + i % (2 * tiles), 0)

    def fill(read, row, out_ref):
        for k in range(4):

            @pl.when(pl.program_id(0) // tiles == k)
            def _():
                out_ref[...] = read(k)

    arrays = [(block, rows_of(k, tiles), part) for k, part in enumerate(parts)]
    return assemble("out_grad", meta, arrays, 4 * tiles, ((4 * rows, cols), block, index), fill)


def finish_in(meta, parts, before=None):
    rows, cols = parts[0][0].shape
    tile, tiles = 256, rows // 256
    skip = 0 if before is None else tiles

    def fill(read, row, out_ref):
        mine, other = read(0), read(1)
        out_ref[:, :cols] = jnp.where(row == 0, mine, other)
        out_ref[:, cols:] = jnp.where(row == 0, other, mine)

    arrays = [((tile, cols), tiled, part) for part in parts]
    out = ((2 * rows, 2 * cols), (tile, 2 * cols), lambda i, *_: (i + skip, 0))
    return assemble("in_grad", meta, arrays, tiles, out, fill, before)


def finish_qkv(meta, parts):
    feats, tile = parts[0][0].shape[1], 256
    blocks = [(2 * HS, tile), (HS, tile)] * 2

    def fill(read, row, out_ref):
        mine, other = (jnp.concatenate([read(k), read(k + 1)], 0).T for k in (0, 2))
        out_ref[:, 0, :] = jnp.where(row == 0, mine, other)
        out_ref[:, 1, :] = jnp.where(row == 0, other, mine)

    arrays = [(block, lambda i, *_: (0, i), part) for block, part in zip(blocks, parts, strict=True)]
    out = ((feats, 2, 3 * HS), (tile, 2, 3 * HS), lambda i, *_: (i, 0, 0))
    return assemble("qkv_grad", meta, arrays, feats // tile, out, fill)


def finish_dense(meta, parts):
    feats = parts[0][0].shape[1]

    def fill(read, row, out_ref):
        out_ref[row] = read(0)
        out_ref[1 - row] = read(1)

    arrays = [((HS, feats), lambda *_: (1, 0), part) for part in parts]
    out = ((2, HS, feats), (2, HS, feats), lambda *_: (0, 0, 0))
    return assemble("dense_grad", meta, arrays, 1, out, fill)


class Names:
    def __getattr__(self, name):
        return name


def is_name(value):
    return isinstance(value, (str, tuple))


class Beats:
    def __init__(self):
        self.env, self.tasks, self.flying = {}, [], []
        self.now, self.token = 0, jnp.zeros((8, LANES), F32)
        self.last, self.new = self.token, []
        self.line = Line()

    def compute(self, beat, names, fn, *inputs, top=False):
        self.tasks.append((beat, inputs, names, (fn, None) if top else fn))

    def send(self, beat, name, fn, source, beats=1):
        self.tasks.append((beat, (source,), name, (fn, beats)))

    def put(self, name, value):
        self.env[name] = value
        self.new.append(name)

    def run(self):
        while self.tasks or self.flying or self.line.busy:
            if self.now > 20 + 8 * self.line.count:
                raise ValueError([task[:3] for task in self.tasks])
            self.line.beat(self)
            for task in [t for t in self.tasks if isinstance(t[3], tuple)] + self.tasks[:]:
                beat, inputs, names, fn = task
                if not any(task is t for t in self.tasks):
                    continue
                if beat > self.now or any(is_name(i) and i not in self.env for i in inputs):
                    continue
                self.tasks = [t for t in self.tasks if t is not task]
                values = [self.env[i] if is_name(i) else i for i in inputs]
                if isinstance(fn, tuple) and fn[1] is None:
                    self.do(names, fn[0], *values)
                elif isinstance(fn, tuple):
                    fn, beats = fn
                    value = fn(tie(values[0], self.token))
                    if beats:
                        self.flying.append((self.now + beats, names, value))
                    else:
                        self.env[names] = value
                else:
                    self.do(names, fn, *values)
            self.tick()

    def do(self, names, fn, first, *rest):
        outs = fn(tie(first, self.last), *rest)
        for name, value in [(names, outs)] if is_name(names) else zip(names, outs, strict=True):
            self.put(name, value)
        self.last = jax.tree.leaves(outs)[0]
        return outs

    def tick(self):
        self.now += 1
        for due, name, value in self.flying:
            if due <= self.now:
                self.put(name, value)
        self.flying = [f for f in self.flying if f[0] > self.now]
        names = list(dict.fromkeys(n for n in self.new if n in self.env))
        values = lax.optimization_barrier((self.token, *[self.env[n] for n in names]))
        self.token = self.last = values[0]
        self.env.update(zip(names, values[1:], strict=True))
        self.new = []


class Line:
    def __init__(self):
        self.count, self.place = lax.axis_size("dp"), lax.axis_index("dp")
        self.mid = self.count // 2
        self.queue, self.going = [], []

    @property
    def busy(self):
        return bool(self.queue or self.going)

    def enter(self, *names):
        self.queue += names

    def on(self, *places):
        return (self.place == places[0]) | (self.place == places[1])

    def pairs(self, step):
        n, mid = self.count, self.mid
        if step < mid - 1:
            return [(step, step + 1), (n - 1 - step, n - 2 - step)]
        if step == mid - 1:
            return [(mid - 1, mid), (mid, mid - 1)]
        step -= mid
        return [(mid - 1 - step, mid - 2 - step), (mid + step, mid + 1 + step)]

    def beat(self, beats):
        env, mid, steps = beats.env, self.mid, 2 * self.mid - 1
        later, outward = [], {}
        for name, step in self.going:
            got, value = (name, step), (name, "held")
            if step + 1 == steps:
                src = self.pairs(step)
                held, arrived = env[value], env[got]
                env[name, "sum"] = jnp.where(self.on(src[0][1], src[1][1]), arrived, held)
                env[name, "parts"] = self.on(src[0][1], src[1][1]), arrived, held
            else:
                later.append((name, step + 1))
        starting = []
        if self.queue and self.queue[0] in env and self.queue[0] != "small":
            starting = [self.queue.pop(0)]
            env[starting[0], "held"] = env[starting[0]]
        small = [n for n in self.queue if n == "small" and n in env]
        for n in small:
            self.queue.remove(n)
            env[n, "held"] = env[n]
            starting.append(n)
        moving = [(n, 0) for n in starting] + later

        def update(name, step):
            if step == 0:
                return (lambda v: v), [(name, "held")]
            inputs = [(name, "held"), (name, step - 1)]
            if step <= mid:
                return add_low, inputs
            src = self.pairs(step - 1)
            return choose(self.on(src[0][1], src[1][1])), inputs

        for name, step in moving:
            match = [
                m
                for m in moving
                if step >= mid
                and m[1] == 2 * mid - 2 - step
                and env[m[0]].shape == env[name].shape
                and m not in outward
            ]
            if match:
                outward[match[0]] = (name, step)
        joint = self.add_jointly(beats, moving, outward)
        for name, step in sorted(moving, key=lambda m: (m[1] != mid - 1, m[1] < mid)):
            if (name, step) in outward or (name, step) in outward.values():
                continue
            if step and (name, step) not in joint:
                fn, inputs = update(name, step)
                beats.do((name, "held"), fn, *[env[i] for i in inputs])
            self.send(beats, self.pairs(step), (name, "held"), [(name, step)])
        for (name, step), (far, far_step) in outward.items():
            if (far, far_step) not in joint:
                fn, inputs = update(name, step)
                if step:
                    beats.do((name, "held"), fn, *[env[i] for i in inputs])
                inputs = update(far, far_step)[1]
                outer = self.on(step, self.count - 1 - step)
                if far_step > mid:
                    gets = self.on(*[pair[1] for pair in self.pairs(far_step - 1)])
                    beats.do((far, "held"), choose(gets), *[env[i] for i in inputs])
                    beats.do((far, "held"), choose(outer), env[far, "held"], env[name, "held"])
                else:
                    add = choose_or_add(outer)
                    beats.do((far, "held"), add, env[name, "held"], *[env[i] for i in inputs])
            self.send(
                beats,
                self.pairs(step) + self.pairs(far_step),
                (far, "held"),
                [(name, step), (far, far_step)],
            )
        self.going = moving

    def add_jointly(self, beats, moving, outward):
        env, mid = beats.env, self.mid
        for far, far_step in moving:
            shape = env[far].shape
            mine = [m for m, step in moving if step == mid - 1 and step and env[m].shape == shape]
            inner = [m for m, out in outward.items() if out == (far, far_step)]
            if far_step != mid or not mine or len(shape) != 2 or (inner and inner[0][1]):
                continue
            keys = [(mine[0], "held"), (far, "held")]
            arrays = [env[mine[0], "held"], env[mine[0], mid - 2], env[far, "held"], env[far, mid - 1]]
            outs, flag = [(shape[1], BF)] * 2, None
            if inner:
                arrays.append(env[inner[0][0], "held"])
                flag = self.on(0, self.count - 1)

            def add(*v):
                a, b, c, d = v[-5:-1] if inner else v
                both = plain_add(a, b) + plain_add(c, d)
                return both[:1] + [jnp.where(v[0], v[-1], both[1])] if inner else both

            beats.do(keys, lambda *v: rowwise(add, shape[0], outs, *v, flag=flag), *arrays)
            return [(mine[0], mid - 1), (far, far_step)]
        return []

    def send(self, beats, pairs, source, gets):
        value = lax.ppermute(tie(beats.env[source], beats.token), "dp", pairs)
        for name, step in gets:
            beats.flying.append((beats.now + 1, (name, step), value))


def per_device(
    residual_in,
    attn_gain,
    attn_shift,
    mlp_gain,
    mlp_shift,
    qkv_weight,
    qkv_bias,
    dense_weight,
    dense_bias,
    in_weight,
    in_bias,
    out_weight,
    out_bias,
    cotangent,
):
    row, col = lax.axis_index("row"), lax.axis_index("col")
    rows, feats = residual_in.shape
    slots, width = lax.axis_size("col"), 2 * feats
    units = in_weight.shape[1] // 2
    other = 1 - row
    plan = Beats()
    env, compute, send, n = plan.env, plan.compute, plan.send, Names()

    def summed(name):
        return name, n.sum


    def below(*parts):
        return jnp.concatenate(parts, 0)

    def part(lo, hi):
        return lambda v: lax.slice_in_dim(v, lo, hi)

    def share(beat, name, fn, source, *needs):
        compute_free = (beat, (source, *needs), name, (fn, 0))
        plan.tasks.append(compute_free)

    env.update(res=residual_in, cot=cotangent)
    env[n.gx] = jnp.stack([attn_gain, attn_shift, mlp_gain, mlp_shift])

    send(0, n.gy, swap_row, n.gx)
    send(0, n.res_x, swap_row, n.res)
    send(0, n.res_y, swap_y, n.res)
    send(0, n.res_c, swap_core, n.res)
    mid = feats // 2
    pick = lax.dynamic_slice
    compute(0, n.in_sent0, lambda w: pick(w, (0, other * units), (mid, units)), in_weight)
    compute(0, n.wx, lambda w: half(w, 1, row), in_weight)
    compute(0, n.ox, lambda w: half(w, 0, row), out_weight)
    compute(0, n.in_sent1, lambda w: pick(w, (mid, other * units), (mid, units)), in_weight)

    compute(0, [n.cos, n.low, n.high], lambda _: rotary_tables(slots * rows), n.gx)

    send(1, n.wy0, swap_row, n.in_sent0)
    send(1, n.res_xy, swap_y, n.res_x)
    send(1, n.res_xc, swap_core, n.res_x)
    send(1, n.res_yc, swap_core, n.res_y)
    compute(1, n.norm0, lambda *a: norm_call(col, 0, *a), n.res, n.res_x, n.gx, n.gy)
    for i in range(2):
        at = other * units + i * (units // 2)
        compute(1, (n.oy_sent, i), lambda w, at=at: pick(w, (at, 0), (units // 2, feats)), out_weight)
    compute(1, n.qx, lambda w: lax.dynamic_index_in_dim(w, row, 1, False), qkv_weight)
    compute(1, n.dense_sent, lambda w: lax.dynamic_index_in_dim(w, other, 0, False), dense_weight)
    compute(1, n.dx, lambda w: lax.dynamic_index_in_dim(w, row, 0, False), dense_weight)

    send(2, n.wy1, swap_row, n.in_sent1)
    send(2, n.res_xyc, swap_core, n.res_xy, 0)

    def gather_col(value):
        return lax.all_gather(value, "col", axis=0, tiled=True)

    share(2, n.g, gather_col, n.cot)

    def norm_rest(res_c, res_xc, res_y, res_xy, res_yc, res_xyc, gx, gy, before):
        before = norm_call(col, 1, res_c, res_xc, gx, gy, *before)
        before = norm_call(col, 2, res_y, res_xy, gx, gy, *before)
        return norm_call(col, 3, res_yc, res_xyc, gx, gy, *before)

    compute(
        2,
        [n.ax, n.ay, n.mx, n.my],
        norm_rest,
        *[n.res_c, n.res_xc, n.res_y, n.res_xy, n.res_yc, n.res_xyc, n.gx, n.gy, n.norm0],
    )

    send(3, n.cot_x, swap_row, n.cot)
    in_bias_mine = lax.dynamic_slice_in_dim(in_bias, row * units, units, 0)
    compute(3, [n.active, n.slope], pre_call, n.mx, n.my, n.wx, n.wy0, n.wy1, in_bias_mine)

    def grads(beat, names, cuts, *inputs, **keys):
        compute(beat, names, lambda *a: weight_grad(cuts, *a, **keys), *inputs)

    two = [units // 2] * 2
    half_units = [units // 2]
    grads(3, [n.out_own0], half_units, n.active, n.g, vmem=58)
    z = 4
    for i in range(2):
        send(z + i, (n.oy, i), swap_row, (n.oy_sent, i))
    oy = [(n.oy, 0), (n.oy, 1)]
    compute(z, [n.out_own1], lambda a, g: weight_grad(half_units, (a, units // 2), g, vmem=58), n.active, n.g)
    share(z, n.h, gather_col, n.cot_x)
    compute(z, n.x_near, below, n.res, n.res_y)
    compute(z, n.y_near, below, n.res_x, n.res_xy)
    compute(z, n.x_far, below, n.res_c, n.res_yc)
    compute(z, n.y_far, below, n.res_xc, n.res_xyc)
    grads(z + 1, [n.out_oth0, n.out_oth1], two, n.active, n.h, vmem=58)
    compute(z + 2, [n.pre_grad, n.in_bias_sum], pre_grad_call, n.g, n.h, n.ox, *oy, n.slope)
    two = [feats // 2] * 2
    grads(z + 3, [n.in_own0, n.in_own1], two, n.mx, n.pre_grad)
    grads(z + 3, [n.in_oth0, n.in_oth1], two, n.my, n.pre_grad)
    cut = 5 * feats // 8
    for i, (lo, hi) in enumerate(((0, cut), (cut, feats))):
        sent = (n.qy_sent, i)
        compute(2, sent, lambda w, lo=lo, hi=hi: lax.dynamic_index_in_dim(w[lo:hi], other, 1, False), qkv_weight)
        send(z + 2 + i, (n.qy, i), swap_row, sent)
    send(z + 3, n.dy, swap_row, n.dense_sent)
    compute(z + 4, n.qy, below, (n.qy, 0), (n.qy, 1))
    qkv_bias_mine = lax.dynamic_index_in_dim(qkv_bias, row, 0, False)
    compute(
        z + 4,
        [n.query, n.key, n.value],
        packed_call,
        *[n.ax, n.ay, n.qx, n.qy, qkv_bias_mine, n.cos, n.low, n.high],
    )
    compute(
        z + 4,
        n.attended_grad,
        lambda g, h, dx, dy: (dot(g, dx, NT) + dot(h, dy, NT)).astype(BF),
        *[n.g, n.h, n.dx, n.dy],
    )
    compute(
        z + 5,
        [n.packed_grad, n.attended, n.qkv_bias_sum],
        lambda *a: attention(slots, *a),
        *[n.query, n.key, n.value, n.attended_grad, n.cos, n.low, n.high],
    )
    cuts = [2 * HS, 2 * HS]
    grads(z + 6, [n.att_own0, n.att_own1], cuts, n.packed_grad, n.ax, n.attended, n.g)
    grads(z + 6, [n.att_oth0, n.att_oth1], cuts, n.packed_grad, n.ay, n.attended, n.h)

    send(z + 4, n.in_oth0_x, swap_row, n.in_oth0)
    send(z + 5, n.in_oth1_x, swap_row, n.in_oth1)
    send(z + 7, n.att_oth0_x, swap_row, n.att_oth0)
    send(z + 8, n.att_oth1_x, swap_row, n.att_oth1)
    plan.line.enter(
        *(n.out_own0, n.out_own1, n.out_oth0, n.out_oth1, n.in_own0, n.in_own1, n.in_oth0_x),
        *(n.att_own0, n.att_own1, n.att_oth0_x, n.att_oth1_x, n.in_oth1_x, n.small),
    )

    def choose_part(parts):
        return choose(parts[0])(parts[2], parts[1])

    compute(z + 5, n.out_oth0_s, choose_part, (n.out_oth0, n.parts))
    compute(z + 6, n.out_oth1_s, choose_part, (n.out_oth1, n.parts))
    send(z + 6, n.out_oth0_y, swap_row, n.out_oth0_s)
    send(z + 9, n.out_oth1_y, swap_row, n.out_oth1_s)

    for beat, part, name, sums, x, y in (
        (z + 7, 1, (n.ng, n.far), n.sums_far, n.x_far, n.y_far),
        (z + 8, 0, (n.ng, n.near), n.sums_near, n.x_near, n.y_near),
    ):
        compute(
            beat,
            [name, sums],
            lambda *a, part=part: norm_grad_call(col, part, *a),
            *[x, y, n.gx, n.gy, n.packed_grad, n.pre_grad, n.qx, n.qy, n.wx, n.wy0, n.wy1],
        )
    for beat, part, name in ((z + 9, 1, (n.mixed, n.far)), (z + 10, 0, (n.mixed, n.near))):
        compute(
            beat,
            name,
            lambda *a, part=part: mixed_call(col, part, *a),
            *[n.attended, n.active, n.dx, n.dy, n.ox, *oy],
        )

    part_rows = rows // 2

    def near_sum(a, b, c):
        out = a.astype(F32) + b.astype(F32) + c.astype(F32)
        return [out[:, feats:].astype(BF), out[:, :feats]]

    outs = [(feats, BF), (feats, F32)]

    def near_part(i, join=False):
        at = i * part_rows

        def fn(a, b, c, *before):
            keys = dict(whole=rows, skip=at, before=before) if join else {}
            return rowwise(near_sum, part_rows, outs, (a, at), (b, at), c, vmem=58, **keys)

        return fn

    def far_sum(i):
        at, outs = rows + i * part_rows, [(width, BF)]
        return lambda a, b: rowwise(plain_add, part_rows, outs, (a, at), (b, at), vmem=58)[0]

    def scatter(beat, name, last=False):
        far, mine, got = [(name, i) for i in (n.far, n.near, n.core)]
        send(beat, got, swap_core, far, 0)
        got_y = [(name, n.near, i) for i in range(2)]
        for i in range(2):
            far_y = (name, n.far, i)
            compute(beat + i, far_y, far_sum(i), mine, got)
            send(beat + 1 + i, got_y[i], swap_y, far_y)
        if last:
            for i in range(2):
                sent = (name, n.sent, i)
                compute(beat + 2 + i, [sent, (name, n.keep, i)], near_part(i), mine, got, got_y[i], top=i == 1)
                send(beat + 3, (name, n.got, i), swap_row, sent)
            return
        half_sent, half_keep = [(name, part, 0) for part in (n.sent, n.keep)]
        compute(beat + 2, [half_sent, half_keep], near_part(0, True), mine, got, got_y[0])
        last_part = [near_part(1, True), mine, got, got_y[1], half_sent, half_keep]
        compute(beat + 3, [(name, n.sent), (name, n.keep)], *last_part, top=True)
        send(beat + 3, (name, n.got), swap_row, (name, n.sent))

    scatter(z + 8, n.ng)
    compute(
        z + 14,
        n.block_out,
        lambda a0, a1, x0, x1, res, b, c: (
            res.astype(F32) + below(a0, a1) + below(x0, x1).astype(F32) + b + c
        ).astype(BF),
        *[(n.mixed, part, i) for part in (n.keep, n.got) for i in range(2)],
        *[n.res, dense_bias, out_bias],
    )

    def own_norm(res, res_x):
        x, y = res.astype(F32), res_x.astype(F32)
        average = (jnp.sum(x, 1, keepdims=True) + jnp.sum(y, 1, keepdims=True)) / width
        squares = (jnp.sum(x * x, 1, keepdims=True) + jnp.sum(y * y, 1, keepdims=True)) / width
        scale = lax.rsqrt(squares - average * average + EPSILON)
        return (x - average) * scale, scale

    def token_sums(keep, xg, res, res_x):
        normed, scale = own_norm(res, res_x)
        grad = keep + xg.astype(F32)
        return jnp.stack([jnp.sum(grad, 1), jnp.sum(grad * normed, 1)])

    compute(z + 12, n.tok, token_sums, (n.ng, n.keep), (n.ng, n.got), n.res, n.res_x)
    send(z + 12, n.tok_x, swap_row, n.tok, 0)

    def finish_input(keep, xg, res, res_x, cot, tok, tok_x):
        normed, scale = own_norm(res, res_x)
        tok = (tok + tok_x) / width
        grad = keep + xg.astype(F32)
        return cot.astype(F32) + scale * (grad - tok[0][:, None] - normed * tok[1][:, None])

    rest = [n.res, n.res_x, n.cot, n.tok, n.tok_x]
    compute(
        z + 12, n.input_grad, finish_input, (n.ng, n.keep), (n.ng, n.got), *rest
    )

    def small_all(near, far, cot, qkv_bias_sum, in_bias_sum):
        bias_sum = jnp.pad(jnp.sum(cot, 0, dtype=F32), (0, feats))
        parts = [(near + far).reshape(-1), bias_sum, qkv_bias_sum.reshape(-1), in_bias_sum.reshape(-1)]
        return jnp.concatenate(parts)

    def take(parts):
        return jnp.where(parts[0], parts[1], parts[2])

    compute(z + 8, n.small, small_all, n.sums_near, n.sums_far, n.cot, n.qkv_bias_sum, n.in_bias_sum)
    compute(z + 12, n.small_s, take, (n.small, n.parts), top=True)
    send(z + 12, n.small_x, swap_row, n.small_s)

    def by_feature(mine, got):
        mine, got = (v[: 5 * width].reshape(5, width) for v in (mine, got))
        return mine[:, :feats] + got[:, feats:]

    compute(z + 13, n.small0, by_feature, n.small_s, n.small_x)
    send(z + 13, n.small0_c, swap_core, n.small0, 0)
    compute(z + 13, n.small1, jnp.add, n.small0, n.small0_c)
    send(z + 13, n.small1_y, swap_y, n.small1, 0)
    compute(z + 13, n.small2, jnp.add, n.small1, n.small1_y)

    def finish(beat, name, fn, *sources):
        def step(*sources):
            flag = next(v[0] for v in sources if isinstance(v, tuple))
            arrays = [v[1:] if isinstance(v, tuple) else (v,) for v in sources]
            return fn(jnp.stack([row, flag.astype(jnp.int32)]), arrays)

        compute(beat, name, step, *sources)

    def done(*names):
        return [(v, n.parts) for v in names]

    finish(z + 11, n.out_weight_grad, finish_out, *done(n.out_own0, n.out_own1), n.out_oth0_y, n.out_oth1_y)
    att = done(n.att_own0, n.att_own1, n.att_oth0_x, n.att_oth1_x)
    finish(z + 13, n.qkv_weight_grad, finish_qkv, *att)
    finish(z + 13, n.dense_weight_grad, finish_dense, att[1], att[3])
    finish(z + 12, n.in_grad0, finish_in, *done(n.in_own0, n.in_oth0_x))

    def second(meta, arrays):
        return finish_in(meta, arrays[:2], arrays[2][0])

    finish(z + 14, n.in_weight_grad, second, *done(n.in_own1, n.in_oth1_x), n.in_grad0)
    scatter(z + 10, n.mixed, last=True)
    plan.run()
    def in_order(mine, got):
        return jnp.where(row == 0, jnp.concatenate([mine, got]), jnp.concatenate([got, mine]))

    by_feature = env[n.small2]
    by_col, by_col_got = (env[name][5 * width :] for name in (n.small_s, n.small_x))
    qkv_bias_grad = in_order(by_col[: 3 * HS], by_col_got[: 3 * HS]).reshape(2, 3 * HS)
    in_bias_grad = in_order(by_col[3 * HS :], by_col_got[3 * HS :])
    return (
        env[n.block_out],
        env[n.input_grad],
        by_feature[0],
        by_feature[1],
        by_feature[2],
        by_feature[3],
        env[n.qkv_weight_grad],
        qkv_bias_grad,
        env[n.dense_weight_grad],
        by_feature[4],
        env[n.in_weight_grad],
        in_bias_grad,
        env[n.out_weight_grad],
        by_feature[4],
    )


def solution(mesh):
    in_specs = (
        P(("dp", "col"), "row"),
        P("row"),
        P("row"),
        P("row"),
        P("row"),
        P("row", "col", None),
        P("col", None),
        P("col", None, "row"),
        P("row"),
        P("row", "col"),
        P("col"),
        P("col", "row"),
        P("row"),
        P(("dp", "col"), "row"),
    )
    out_specs = (
        P(("dp", "col"), "row"),
        P(("dp", "col"), "row"),
        P("row"),
        P("row"),
        P("row"),
        P("row"),
        P("row", "col", None),
        P("col", None),
        P("col", None, "row"),
        P("row"),
        P("row", "col"),
        P("col"),
        P("col", "row"),
        P("row"),
    )
    return jax.shard_map(
        per_device, mesh=mesh, in_specs=in_specs, out_specs=out_specs, check_vma=False
    )
```

```python
import math

import jax
import jax.numpy as jnp
from jax import lax
from jax.experimental import pallas as pl
from jax.experimental.pallas import tpu as pltpu
from jax.sharding import PartitionSpec as P

HS = 256
ROT = 64
LENGTH = 2048
LANES = 128
EPSILON = 1e-05
ROPE_BASE = 10000.0
NEGATIVE = -1e30
BF = jnp.bfloat16
F32 = jnp.float32
NN, NT, TN = ((1,), (0,)), ((1,), (1,)), ((0,), (0,))
MIB = 2**20
COST = pl.CostEstimate(flops=0, bytes_accessed=0, transcendentals=0)


def tie(value, *others):
    return lax.optimization_barrier((value,) + others)[0]


def swap_row(value):
    return lax.ppermute(value, "row", [(0, 1), (1, 0)])


def swap_col(value, bit):
    return lax.ppermute(value, "col", [(i, i ^ bit) for i in range(lax.axis_size("col"))])


def swap_y(value):
    return swap_col(value, 2)


def swap_core(value):
    return swap_col(value, 1)


def half(array, axis, index):
    size = array.shape[axis] // 2
    return lax.dynamic_slice_in_dim(array, index * size, size, axis)


def dot(a, b, dims):
    return lax.dot_general(a, b, (dims, ((), ())), preferred_element_type=F32)


def rotary_tables(tokens):
    position = (jnp.arange(tokens) % LENGTH).astype(F32)
    lane = jnp.arange(LANES)
    index = (lane % (ROT // 2)).astype(F32)
    frequency = ROPE_BASE ** (-(2.0 * index) / ROT)
    angle = position[:, None] * frequency[None, :]
    cos = jnp.where(lane < ROT, jnp.cos(angle), 1.0)
    sin = jnp.sin(angle)
    low = jnp.where(lane < ROT // 2, -sin, 0.0)
    high = jnp.where((lane >= ROT // 2) & (lane < ROT), sin, 0.0)
    return cos, low, high


def rotate(values, cos, low, high):
    first = values[:, :LANES]
    up = pltpu.roll(first, LANES - ROT // 2, 1)
    down = pltpu.roll(first, ROT // 2, 1)
    first = first * cos + up * low + down * high
    return jnp.concatenate([first, values[:, LANES:]], 1)


def tiled(i, *_):
    return (i, 0)


def fixed(*_):
    return (0, 0)


def call(kernel, name, steps, ins, outs, col=None, vmem=28, tile=None):
    def block(shape, index, rows=None):
        rows = rows or (shape[0] if index is fixed else tile or shape[0] // steps)
        return pl.BlockSpec((rows, shape[1]), index)

    spec = pltpu.PrefetchScalarGridSpec(
        num_scalar_prefetch=0 if col is None else 1,
        grid=(steps,),
        in_specs=[block(a.shape, index) for a, index in ins],
        out_specs=tuple(block(shape, index, rows) for shape, _, rows, index in outs),
    )
    return pl.pallas_call(
        kernel if col is None else lambda _, *refs: kernel(*refs),
        grid_spec=spec,
        out_shape=tuple(jax.ShapeDtypeStruct(shape, dtype) for shape, dtype, _, _ in outs),
        compiler_params=pltpu.CompilerParams(vmem_limit_bytes=vmem * MIB),
        cost_estimate=COST,
        name=name,
    )(*([] if col is None else [col.reshape(1)]), *[a for a, _ in ins])


def normed_halves(x_ref, y_ref):
    x, y = x_ref[...].astype(F32), y_ref[...].astype(F32)
    width = x.shape[1] + y.shape[1]
    average = (jnp.sum(x, 1, keepdims=True) + jnp.sum(y, 1, keepdims=True)) / width
    squares = (jnp.sum(x * x, 1, keepdims=True) + jnp.sum(y * y, 1, keepdims=True)) / width
    scale = lax.rsqrt(squares - average * average + EPSILON)
    return (x - average) * scale, (y - average) * scale


def norm_kernel(x_ref, y_ref, gx_ref, gy_ref, ax_ref, ay_ref, mx_ref, my_ref):
    x, y = normed_halves(x_ref, y_ref)
    ax_ref[...] = (x * gx_ref[0:1] + gx_ref[1:2]).astype(BF)
    ay_ref[...] = (y * gy_ref[0:1] + gy_ref[1:2]).astype(BF)
    mx_ref[...] = (x * gx_ref[2:3] + gx_ref[3:4]).astype(BF)
    my_ref[...] = (y * gy_ref[2:3] + gy_ref[3:4]).astype(BF)


def norm_call(col, flip, x, y, gx, gy, *before):
    (rows, feats), tile, slots = x.shape, 256, 4
    steps = rows // tile

    def index(i, col_ref):
        return ((col_ref[0] ^ flip) * steps + i, 0)

    rest = [pl.BlockSpec(memory_space=pl.ANY)] * len(before)
    block = pl.BlockSpec((tile, feats), tiled)
    whole = pl.BlockSpec(gx.shape, fixed)
    return pl.pallas_call(
        lambda _, x, y, gx, gy, *refs: norm_kernel(x, y, gx, gy, *refs[len(before) :]),
        grid_spec=pltpu.PrefetchScalarGridSpec(
            num_scalar_prefetch=1,
            grid=(steps,),
            in_specs=[block, block, whole, whole] + rest,
            out_specs=(pl.BlockSpec((tile, feats), index),) * 4,
        ),
        out_shape=(jax.ShapeDtypeStruct((slots * rows, feats), BF),) * 4,
        input_output_aliases={5 + i: i for i in range(len(before))},
        compiler_params=pltpu.CompilerParams(vmem_limit_bytes=58 * MIB),
        cost_estimate=COST,
        name="norm",
    )(col.reshape(1), x, y, gx, gy, *before)


def pre_kernel(x_ref, y_ref, wx_ref, wy0_ref, wy1_ref, bias_ref, active_ref, slope_ref):
    mid, part = wy0_ref.shape[0], wx_ref.shape[1]
    for start in range(0, wx_ref.shape[1], part):
        at = slice(start, start + part)
        u = dot(x_ref[...], wx_ref[:, at], NN) + bias_ref[:, at]
        u = u + dot(y_ref[:, :mid], wy0_ref[:, at], NN) + dot(y_ref[:, mid:], wy1_ref[:, at], NN)
        phi = 0.5 * (1.0 + lax.erf(u * 2.0**-0.5))
        bell = jnp.exp(-0.5 * u * u)
        active_ref[:, at] = (u * phi).astype(BF)
        slope_ref[:, at] = (phi + u * bell * (2.0 * math.pi) ** (-0.5)).astype(BF)


def pre_call(x, y, wx, wy0, wy1, bias):
    tokens, tile, units = x.shape[0], 256, wx.shape[1]
    return call(
        pre_kernel,
        "pre_act",
        tokens // tile,
        [(x, tiled), (y, tiled), (wx, fixed), (wy0, fixed), (wy1, fixed), (bias.reshape(1, -1), fixed)],
        [((tokens, units), BF, tile, tiled)] * 2,
        vmem=58,
    )


def rowwise(fn, rows, outs, *ins, flag=None, vmem=20, whole=None, skip=0, before=()):
    tile = 256
    ins = [i if isinstance(i, tuple) else (i, 0) for i in ins]
    flags = [] if flag is None else [flag.astype(jnp.int32).reshape(1)]

    def at(first):
        return fixed if first is None else lambda i, *_: (i + first // tile, 0)

    def kernel(*refs):
        values = [ref[0] != 0 for ref in refs[: len(flags)]]
        refs = refs[len(flags) :]
        results = fn(*values, *[ref[...] for ref in refs[: len(ins)]])
        for ref, result in zip(refs[len(ins) + len(before) :], results, strict=True):
            ref[...] = result

    first_in = len(flags) + len(ins)
    return pl.pallas_call(
        kernel,
        grid_spec=pltpu.PrefetchScalarGridSpec(
            num_scalar_prefetch=len(flags),
            grid=(rows // tile,),
            in_specs=[pl.BlockSpec((tile, a.shape[1]), at(first)) for a, first in ins]
            + [pl.BlockSpec(memory_space=pl.ANY)] * len(before),
            out_specs=tuple(pl.BlockSpec((tile, cols), at(skip)) for cols, _ in outs),
        ),
        out_shape=tuple(jax.ShapeDtypeStruct((whole or rows, cols), dtype) for cols, dtype in outs),
        input_output_aliases={first_in + i: i for i in range(len(before))},
        compiler_params=pltpu.CompilerParams(vmem_limit_bytes=vmem * MIB),
        cost_estimate=COST,
        name="rowwise",
    )(*flags, *[a for a, _ in ins], *before)


def plain_add(a, b):
    return [(a.astype(F32) + b.astype(F32)).astype(BF)]


def add_low(a, b):
    return (a.astype(F32) + b.astype(F32)).astype(a.dtype)


def choose(flag):
    def fn(held, arrived):
        if held.ndim == 1:
            return jnp.where(flag, arrived, held)
        outs = [(held.shape[1], BF)]
        return rowwise(lambda f, h, a: [jnp.where(f, a, h)], held.shape[0], outs, held, arrived, flag=flag)[0]

    return fn


def choose_or_add(flag):
    return lambda value, a, b: jnp.where(flag, value, add_low(a, b))


def weight_grad(cuts, a, b, last_a=None, last_b=None, vmem=20):
    tokens, cols, tile = b.shape[0], b.shape[1], 256
    own = sum(cuts) // tile if last_a is None else a.shape[1] // tile
    skip = 0
    if isinstance(a, tuple):
        a, skip = a[0], a[1] // tile
    first = [sum(cuts[:i]) // tile for i in range(len(cuts) + 1)]

    def kernel(*refs):
        step = pl.program_id(0)

        def store(out):
            for start, end, ref in zip(first[:-1], first[1:], refs[-len(cuts) :], strict=True):

                @pl.when((step >= start) & (step < end))
                def _():
                    ref[...] = out

        if last_a is None:
            store(dot(refs[0][...], refs[1][...], TN).astype(BF))
            return

        @pl.when(step < own)
        def _():
            store(dot(refs[0][...], refs[1][...], TN).astype(BF))

        @pl.when(step >= own)
        def _():
            store(dot(refs[2][...], refs[3][...], TN).astype(BF))

    def index(start, end):
        return lambda i: (jnp.clip(i - start, 0, end - start - 1), 0)

    ins = [a, b] if last_a is None else [a, b, last_a, last_b]
    specs = [
        pl.BlockSpec((tokens, tile), lambda i: (0, jnp.minimum(i, own - 1) + skip)),
        pl.BlockSpec(b.shape, fixed),
        pl.BlockSpec((tokens, tile), fixed),
        pl.BlockSpec(b.shape, fixed),
    ]
    return pl.pallas_call(
        kernel,
        grid=(first[-1],),
        out_shape=tuple(jax.ShapeDtypeStruct((size, cols), BF) for size in cuts),
        in_specs=specs[: len(ins)],
        out_specs=tuple(
            pl.BlockSpec((tile, cols), index(s, e)) for s, e in zip(first[:-1], first[1:], strict=True)
        ),
        compiler_params=pltpu.CompilerParams(vmem_limit_bytes=vmem * MIB),
        cost_estimate=COST,
        name="weight_grad",
    )(*ins)


def pre_grad_kernel(gx_ref, gy_ref, wx_ref, wy0_ref, wy1_ref, slope_ref, out_ref, sum_ref):
    @pl.when(pl.program_id(0) == 0)
    def _():
        sum_ref[...] = jnp.zeros_like(sum_ref)

    mid = wy0_ref.shape[0]
    for i, wy_ref in enumerate((wy0_ref, wy1_ref)):
        at = slice(i * mid, (i + 1) * mid)
        u = dot(gx_ref[...], wx_ref[at, :], NT) + dot(gy_ref[...], wy_ref[...], NT)
        low = (u * slope_ref[:, at].astype(F32)).astype(BF)
        out_ref[:, at] = low
        sum_ref[:, at] += jnp.sum(low.astype(F32), 0, keepdims=True)


def pre_grad_call(gx, gy, wx, wy0, wy1, slope):
    tokens, tile, units = gx.shape[0], 512, wx.shape[0]
    return call(
        pre_grad_kernel,
        "pre_grad",
        tokens // tile,
        [(gx, tiled), (gy, tiled), (wx, fixed), (wy0, fixed), (wy1, fixed), (slope, tiled)],
        [((tokens, units), BF, tile, tiled), ((1, units), F32, 1, fixed)],
    )


def packed_kernel(x_ref, y_ref, wx_ref, wy_ref, bias_ref, cos_ref, low_ref, high_ref, q_ref, k_ref, v_ref):
    out = dot(x_ref[...], wx_ref[...], NN) + dot(y_ref[...], wy_ref[...], NN) + bias_ref[...]
    tables = cos_ref[...], low_ref[...], high_ref[...]
    q_ref[...] = rotate(out[:, :HS], *tables).astype(BF)
    k_ref[...] = rotate(out[:, HS : 2 * HS], *tables).astype(BF)
    v_ref[...] = out[:, 2 * HS :].astype(BF)


def packed_call(x, y, wx, wy, bias, *tables):
    tokens, tile = x.shape[0], 512
    return call(
        packed_kernel,
        "packed",
        tokens // tile,
        [(x, tiled), (y, tiled), (wx, fixed), (wy, fixed), (bias.reshape(1, -1), fixed)]
        + [(t, tiled) for t in tables],
        [((tokens, HS), BF, tile, tiled)] * 3,
    )


def attention_kernel(
    q_ref, k_ref, v_ref, g_ref, cos_ref, low_ref, high_ref, o_ref, out_ref, sum_ref, dk_acc, dv_acc
):
    slots, rows, _ = q_ref.shape
    scale = HS ** (-0.5)
    mask = lax.broadcasted_iota(jnp.int32, (rows, rows), 1) <= lax.broadcasted_iota(
        jnp.int32, (rows, rows), 0
    )
    total_sum = [jnp.zeros((1, HS), F32) for _ in range(3)]

    def unrotate(values, at):
        return rotate(values, cos_ref[at], -low_ref[at], -high_ref[at]).astype(BF)

    for i in range(slots):
        q, g = q_ref[i], g_ref[i]
        scores = []
        for j in range(i + 1):
            s = dot(q, k_ref[j], NT) * scale
            scores.append(jnp.where(mask, s, NEGATIVE) if j == i else s)
        top = scores[0].max(-1, keepdims=True)
        for s in scores[1:]:
            top = jnp.maximum(top, s.max(-1, keepdims=True))
        exps = [jnp.exp(s - top) for s in scores]
        inv = 1.0 / sum(e.sum(-1, keepdims=True) for e in exps)
        probs = [e * inv for e in exps]
        out = jnp.zeros((rows, HS), F32)
        center = jnp.zeros((rows, 1), F32)
        prob_grads = []
        for j in range(i + 1):
            low = probs[j].astype(BF)
            v = v_ref[j]
            out = out + dot(low, v, NN)
            pg = dot(g, v, NT)
            center = center + (probs[j] * pg).sum(-1, keepdims=True)
            prob_grads.append(pg)
            dv = dot(low, g, TN)
            if j == i:
                dv_acc[j] = dv
            else:
                dv_acc[j] += dv
        o_ref[i] = out.astype(BF)
        dq = jnp.zeros((rows, HS), F32)
        for j in range(i + 1):
            sg = (probs[j] * (prob_grads[j] - center)).astype(BF)
            dq = dq + dot(sg, k_ref[j], NN)
            dk = dot(sg, q, TN)
            if j == i:
                dk_acc[j] = dk
            else:
                dk_acc[j] += dk
        dq = unrotate(dq * scale, i)
        out_ref[i, :, 0:HS] = dq
        total_sum[0] = total_sum[0] + jnp.sum(dq.astype(F32), 0, keepdims=True)
    for j in range(slots):
        dk = unrotate(dk_acc[j] * scale, j)
        dv = dv_acc[j].astype(BF)
        out_ref[j, :, HS : 2 * HS] = dk
        out_ref[j, :, 2 * HS :] = dv
        total_sum[1] = total_sum[1] + jnp.sum(dk.astype(F32), 0, keepdims=True)
        total_sum[2] = total_sum[2] + jnp.sum(dv.astype(F32), 0, keepdims=True)
    for i in range(3):
        sum_ref[:, i * HS : (i + 1) * HS] = total_sum[i]


def attention(slots, q, k, v, g, cos, low, high):
    tokens = q.shape[0]
    rows = tokens // slots
    vmem = pl.BlockSpec(memory_space=pltpu.VMEM)
    attended, packed_grad, sums = pl.pallas_call(
        attention_kernel,
        out_shape=(
            jax.ShapeDtypeStruct((slots, rows, HS), BF),
            jax.ShapeDtypeStruct((slots, rows, 3 * HS), BF),
            jax.ShapeDtypeStruct((1, 3 * HS), F32),
        ),
        in_specs=[vmem] * 7,
        out_specs=(vmem,) * 3,
        scratch_shapes=[pltpu.VMEM((slots, rows, HS), F32)] * 2,
        compiler_params=pltpu.CompilerParams(vmem_limit_bytes=48 * MIB),
        cost_estimate=COST,
        name="attention",
    )(*[a.reshape(slots, rows, a.shape[1]) for a in (q, k, v, g, cos, low, high)])
    return packed_grad.reshape(tokens, 3 * HS), attended.reshape(tokens, HS), sums


def mixed_kernel(a_ref, b_ref, dx_ref, dy_ref, wx_ref, wy0_ref, wy1_ref, out_ref):
    feats, mid = dx_ref.shape[1], wy0_ref.shape[0]
    a, b = a_ref[...], b_ref[...]
    out_ref[:, :feats] = (dot(a, dx_ref[...], NN) + dot(b, wx_ref[...], NN)).astype(BF)
    y = dot(a, dy_ref[...], NN) + dot(b[:, :mid], wy0_ref[...], NN) + dot(b[:, mid:], wy1_ref[...], NN)
    out_ref[:, feats:] = y.astype(BF)


def mixed_call(col, part, attended, active, dx, dy, *weights):
    tokens, tile, width = attended.shape[0] // 2, 256, dx.shape[1] + dy.shape[1]
    steps = tokens // tile
    each = steps // 2

    def order(i, col_ref):
        return ((col_ref[0] ^ part ^ (2 * (i // each))) * each + i % each, 0)

    ins = [(attended, order), (active, order)] + [(w, fixed) for w in (dx, dy, *weights)]
    outs = [((tokens, width), BF, tile, tiled)]
    return call(mixed_kernel, "mixed", steps, ins, outs, col, tile=tile)[0]


def norm_grad_kernel(
    x_ref, y_ref, gx_ref, gy_ref, p_ref, u_ref, qx_ref, qy_ref, wx_ref, wy0_ref, wy1_ref, out_ref, sum_ref
):
    feats, mid = x_ref.shape[1], wy0_ref.shape[0]

    @pl.when(pl.program_id(0) == 0)
    def _():
        sum_ref[...] = jnp.zeros_like(sum_ref)

    normed = normed_halves(x_ref, y_ref)
    p, u = p_ref[...], u_ref[...]
    for start in range(0, 2 * feats, mid):
        side, lo = divmod(start, feats)
        at, part = slice(start, start + mid), slice(lo, lo + mid)
        q = (qx_ref, qy_ref)[side][part, :]
        w = wx_ref[part, :] if side == 0 else (wy0_ref, wy1_ref)[lo // mid][...]
        gains = (gx_ref, gy_ref)[side][:, part]
        n = normed[side][:, part]
        a, m = dot(p, q, NT), dot(u, w, NT)
        out_ref[:, at] = (a * gains[0:1] + m * gains[2:3]).astype(BF)
        sum_ref[0:1, at] += jnp.sum(a * n, 0, keepdims=True)
        sum_ref[1:2, at] += jnp.sum(a, 0, keepdims=True)
        sum_ref[2:3, at] += jnp.sum(m * n, 0, keepdims=True)
        sum_ref[3:4, at] += jnp.sum(m, 0, keepdims=True)


def norm_grad_call(col, part, x, y, gx, gy, packed_grad, pre_grad, *weights):
    tokens, tile, width = x.shape[0], 256, x.shape[1] + y.shape[1]
    steps = tokens // tile
    each = steps // 2

    def order(i, col_ref):
        return ((col_ref[0] ^ part ^ (2 * (i // each))) * each + i % each, 0)

    ins = [(x, tiled), (y, tiled), (gx, fixed), (gy, fixed), (packed_grad, order), (pre_grad, order)]
    return call(
        norm_grad_kernel,
        "norm_grad",
        steps,
        ins + [(w, fixed) for w in weights],
        [((tokens, width), BF, tile, tiled), ((4, width), F32, 4, fixed)],
        col,
        vmem=58,
        tile=tile,
    )


def assemble(name, meta, arrays, steps, out, fill, before=None):
    flat = [a for _, _, part in arrays for a in part]
    rest = [] if before is None else [before]
    shape, block, index = out

    def kernel(meta_ref, *refs):
        at = iter(refs[:-1])
        parts = [[next(at) for _ in part] for _, _, part in arrays]

        def read(i):
            values = [ref[...] for ref in parts[i]]
            value = values[0] if len(values) == 1 else jnp.where(meta_ref[1] != 0, *values)
            return value.astype(F32)

        fill(read, meta_ref[0], refs[-1])

    return pl.pallas_call(
        kernel,
        grid_spec=pltpu.PrefetchScalarGridSpec(
            num_scalar_prefetch=1,
            grid=(steps,),
            in_specs=[pl.BlockSpec(block, index) for block, index, part in arrays for _ in part]
            + [pl.BlockSpec(memory_space=pl.ANY)] * len(rest),
            out_specs=pl.BlockSpec(block, index),
        ),
        out_shape=jax.ShapeDtypeStruct(shape, F32),
        input_output_aliases={1 + len(flat): 0} if rest else {},
        compiler_params=pltpu.CompilerParams(vmem_limit_bytes=58 * MIB),
        cost_estimate=COST,
        name=name,
    )(meta, *flat, *rest)


def rows_of(part, tiles):
    return lambda i, *_: (jnp.clip(i - part * tiles, 0, tiles - 1), 0)


def finish_out(meta, parts):
    rows, cols = parts[0][0].shape
    tile, tiles = 256, rows // 256
    block = (tile, cols)

    def index(i, meta_ref):
        return ((i // (2 * tiles) ^ meta_ref[0]) * 2 * tiles + i % (2 * tiles), 0)

    def fill(read, row, out_ref):
        for k in range(4):

            @pl.when(pl.program_id(0) // tiles == k)
            def _():
                out_ref[...] = read(k)

    arrays = [(block, rows_of(k, tiles), part) for k, part in enumerate(parts)]
    return assemble("out_grad", meta, arrays, 4 * tiles, ((4 * rows, cols), block, index), fill)


def finish_in(meta, parts, before=None):
    rows, cols = parts[0][0].shape
    tile, tiles = 256, rows // 256
    skip = 0 if before is None else tiles

    def fill(read, row, out_ref):
        mine, other = read(0), read(1)
        out_ref[:, :cols] = jnp.where(row == 0, mine, other)
        out_ref[:, cols:] = jnp.where(row == 0, other, mine)

    arrays = [((tile, cols), tiled, part) for part in parts]
    out = ((2 * rows, 2 * cols), (tile, 2 * cols), lambda i, *_: (i + skip, 0))
    return assemble("in_grad", meta, arrays, tiles, out, fill, before)


def finish_qkv(meta, parts):
    feats, tile = parts[0][0].shape[1], 256
    blocks = [(2 * HS, tile), (HS, tile)] * 2

    def fill(read, row, out_ref):
        mine, other = (jnp.concatenate([read(k), read(k + 1)], 0).T for k in (0, 2))
        out_ref[:, 0, :] = jnp.where(row == 0, mine, other)
        out_ref[:, 1, :] = jnp.where(row == 0, other, mine)

    arrays = [(block, lambda i, *_: (0, i), part) for block, part in zip(blocks, parts, strict=True)]
    out = ((feats, 2, 3 * HS), (tile, 2, 3 * HS), lambda i, *_: (i, 0, 0))
    return assemble("qkv_grad", meta, arrays, feats // tile, out, fill)


def finish_dense(meta, parts):
    feats = parts[0][0].shape[1]

    def fill(read, row, out_ref):
        out_ref[row] = read(0)
        out_ref[1 - row] = read(1)

    arrays = [((HS, feats), lambda *_: (1, 0), part) for part in parts]
    out = ((2, HS, feats), (2, HS, feats), lambda *_: (0, 0, 0))
    return assemble("dense_grad", meta, arrays, 1, out, fill)


class Names:
    def __getattr__(self, name):
        return name


def is_name(value):
    return isinstance(value, (str, tuple))


class Beats:
    def __init__(self):
        self.env, self.tasks, self.flying = {}, [], []
        self.now, self.token = 0, jnp.zeros((8, LANES), F32)
        self.last, self.new = self.token, []
        self.line = Line()

    def compute(self, beat, names, fn, *inputs, top=False):
        self.tasks.append((beat, inputs, names, (fn, None) if top else fn))

    def send(self, beat, name, fn, source, beats=1):
        self.tasks.append((beat, (source,), name, (fn, beats)))

    def put(self, name, value):
        self.env[name] = value
        self.new.append(name)

    def run(self):
        while self.tasks or self.flying or self.line.busy:
            if self.now > 20 + 8 * self.line.count:
                raise ValueError([task[:3] for task in self.tasks])
            self.line.beat(self)
            for task in [t for t in self.tasks if isinstance(t[3], tuple)] + self.tasks[:]:
                beat, inputs, names, fn = task
                if not any(task is t for t in self.tasks):
                    continue
                if beat > self.now or any(is_name(i) and i not in self.env for i in inputs):
                    continue
                self.tasks = [t for t in self.tasks if t is not task]
                values = [self.env[i] if is_name(i) else i for i in inputs]
                if isinstance(fn, tuple) and fn[1] is None:
                    self.do(names, fn[0], *values)
                elif isinstance(fn, tuple):
                    fn, beats = fn
                    value = fn(tie(values[0], self.token))
                    if beats:
                        self.flying.append((self.now + beats, names, value))
                    else:
                        self.env[names] = value
                else:
                    self.do(names, fn, *values)
            self.tick()

    def do(self, names, fn, first, *rest):
        outs = fn(tie(first, self.last), *rest)
        for name, value in [(names, outs)] if is_name(names) else zip(names, outs, strict=True):
            self.put(name, value)
        self.last = jax.tree.leaves(outs)[0]
        return outs

    def tick(self):
        self.now += 1
        for due, name, value in self.flying:
            if due <= self.now:
                self.put(name, value)
        self.flying = [f for f in self.flying if f[0] > self.now]
        names = list(dict.fromkeys(n for n in self.new if n in self.env))
        values = lax.optimization_barrier((self.token, *[self.env[n] for n in names]))
        self.token = self.last = values[0]
        self.env.update(zip(names, values[1:], strict=True))
        self.new = []


class Line:
    def __init__(self):
        self.count, self.place = lax.axis_size("dp"), lax.axis_index("dp")
        self.mid = self.count // 2
        self.queue, self.going = [], []

    @property
    def busy(self):
        return bool(self.queue or self.going)

    def enter(self, *names):
        self.queue += names

    def on(self, *places):
        return (self.place == places[0]) | (self.place == places[1])

    def pairs(self, step):
        n, mid = self.count, self.mid
        if step < mid - 1:
            return [(step, step + 1), (n - 1 - step, n - 2 - step)]
        if step == mid - 1:
            return [(mid - 1, mid), (mid, mid - 1)]
        step -= mid
        return [(mid - 1 - step, mid - 2 - step), (mid + step, mid + 1 + step)]

    def beat(self, beats):
        env, mid, steps = beats.env, self.mid, 2 * self.mid - 1
        later, outward = [], {}
        for name, step in self.going:
            got, value = (name, step), (name, "held")
            if step + 1 == steps:
                src = self.pairs(step)
                held, arrived = env[value], env[got]
                env[name, "sum"] = jnp.where(self.on(src[0][1], src[1][1]), arrived, held)
                env[name, "parts"] = self.on(src[0][1], src[1][1]), arrived, held
            else:
                later.append((name, step + 1))
        starting = []
        if self.queue and self.queue[0] in env and self.queue[0] != "small":
            starting = [self.queue.pop(0)]
            env[starting[0], "held"] = env[starting[0]]
        small = [n for n in self.queue if n == "small" and n in env]
        for n in small:
            self.queue.remove(n)
            env[n, "held"] = env[n]
            starting.append(n)
        moving = [(n, 0) for n in starting] + later

        def update(name, step):
            if step == 0:
                return (lambda v: v), [(name, "held")]
            inputs = [(name, "held"), (name, step - 1)]
            if step <= mid:
                return add_low, inputs
            src = self.pairs(step - 1)
            return choose(self.on(src[0][1], src[1][1])), inputs

        for name, step in moving:
            match = [
                m
                for m in moving
                if step >= mid
                and m[1] == 2 * mid - 2 - step
                and env[m[0]].shape == env[name].shape
                and m not in outward
            ]
            if match:
                outward[match[0]] = (name, step)
        joint = self.add_jointly(beats, moving, outward)
        for name, step in sorted(moving, key=lambda m: (m[1] != mid - 1, m[1] < mid)):
            if (name, step) in outward or (name, step) in outward.values():
                continue
            if step and (name, step) not in joint:
                fn, inputs = update(name, step)
                beats.do((name, "held"), fn, *[env[i] for i in inputs])
            self.send(beats, self.pairs(step), (name, "held"), [(name, step)])
        for (name, step), (far, far_step) in outward.items():
            if (far, far_step) not in joint:
                fn, inputs = update(name, step)
                if step:
                    beats.do((name, "held"), fn, *[env[i] for i in inputs])
                inputs = update(far, far_step)[1]
                outer = self.on(step, self.count - 1 - step)
                if far_step > mid:
                    gets = self.on(*[pair[1] for pair in self.pairs(far_step - 1)])
                    beats.do((far, "held"), choose(gets), *[env[i] for i in inputs])
                    beats.do((far, "held"), choose(outer), env[far, "held"], env[name, "held"])
                else:
                    add = choose_or_add(outer)
                    beats.do((far, "held"), add, env[name, "held"], *[env[i] for i in inputs])
            self.send(
                beats,
                self.pairs(step) + self.pairs(far_step),
                (far, "held"),
                [(name, step), (far, far_step)],
            )
        self.going = moving

    def add_jointly(self, beats, moving, outward):
        env, mid = beats.env, self.mid
        for far, far_step in moving:
            shape = env[far].shape
            mine = [m for m, step in moving if step == mid - 1 and step and env[m].shape == shape]
            inner = [m for m, out in outward.items() if out == (far, far_step)]
            if far_step != mid or not mine or len(shape) != 2 or (inner and inner[0][1]):
                continue
            keys = [(mine[0], "held"), (far, "held")]
            arrays = [env[mine[0], "held"], env[mine[0], mid - 2], env[far, "held"], env[far, mid - 1]]
            outs, flag = [(shape[1], BF)] * 2, None
            if inner:
                arrays.append(env[inner[0][0], "held"])
                flag = self.on(0, self.count - 1)

            def add(*v):
                a, b, c, d = v[-5:-1] if inner else v
                both = plain_add(a, b) + plain_add(c, d)
                return both[:1] + [jnp.where(v[0], v[-1], both[1])] if inner else both

            beats.do(keys, lambda *v: rowwise(add, shape[0], outs, *v, flag=flag), *arrays)
            return [(mine[0], mid - 1), (far, far_step)]
        return []

    def send(self, beats, pairs, source, gets):
        value = lax.ppermute(tie(beats.env[source], beats.token), "dp", pairs)
        for name, step in gets:
            beats.flying.append((beats.now + 1, (name, step), value))


def per_device(
    residual_in,
    attn_gain,
    attn_shift,
    mlp_gain,
    mlp_shift,
    qkv_weight,
    qkv_bias,
    dense_weight,
    dense_bias,
    in_weight,
    in_bias,
    out_weight,
    out_bias,
    cotangent,
):
    row, col = lax.axis_index("row"), lax.axis_index("col")
    rows, feats = residual_in.shape
    slots, width = lax.axis_size("col"), 2 * feats
    units = in_weight.shape[1] // 2
    other = 1 - row
    plan = Beats()
    env, compute, send, n = plan.env, plan.compute, plan.send, Names()

    def summed(name):
        return name, n.sum


    def below(*parts):
        return jnp.concatenate(parts, 0)

    def part(lo, hi):
        return lambda v: lax.slice_in_dim(v, lo, hi)

    def share(beat, name, fn, source, *needs):
        compute_free = (beat, (source, *needs), name, (fn, 0))
        plan.tasks.append(compute_free)

    env.update(res=residual_in, cot=cotangent)
    env[n.gx] = jnp.stack([attn_gain, attn_shift, mlp_gain, mlp_shift])

    send(0, n.gy, swap_row, n.gx)
    send(0, n.res_x, swap_row, n.res)
    send(0, n.res_y, swap_y, n.res)
    send(0, n.res_c, swap_core, n.res)
    mid = feats // 2
    pick = lax.dynamic_slice
    compute(0, n.in_sent0, lambda w: pick(w, (0, other * units), (mid, units)), in_weight)
    compute(0, n.wx, lambda w: half(w, 1, row), in_weight)
    compute(0, n.ox, lambda w: half(w, 0, row), out_weight)
    compute(0, n.in_sent1, lambda w: pick(w, (mid, other * units), (mid, units)), in_weight)

    compute(0, [n.cos, n.low, n.high], lambda _: rotary_tables(slots * rows), n.gx)

    send(1, n.wy0, swap_row, n.in_sent0)
    send(1, n.res_xy, swap_y, n.res_x)
    send(1, n.res_xc, swap_core, n.res_x)
    send(1, n.res_yc, swap_core, n.res_y)
    compute(1, n.norm0, lambda *a: norm_call(col, 0, *a), n.res, n.res_x, n.gx, n.gy)
    for i in range(2):
        at = other * units + i * (units // 2)
        compute(1, (n.oy_sent, i), lambda w, at=at: pick(w, (at, 0), (units // 2, feats)), out_weight)
    compute(1, n.qx, lambda w: lax.dynamic_index_in_dim(w, row, 1, False), qkv_weight)
    compute(1, n.dense_sent, lambda w: lax.dynamic_index_in_dim(w, other, 0, False), dense_weight)
    compute(1, n.dx, lambda w: lax.dynamic_index_in_dim(w, row, 0, False), dense_weight)

    send(2, n.wy1, swap_row, n.in_sent1)
    send(2, n.res_xyc, swap_core, n.res_xy, 0)

    def gather_col(value):
        return lax.all_gather(value, "col", axis=0, tiled=True)

    share(2, n.g, gather_col, n.cot)

    def norm_rest(res_c, res_xc, res_y, res_xy, res_yc, res_xyc, gx, gy, before):
        before = norm_call(col, 1, res_c, res_xc, gx, gy, *before)
        before = norm_call(col, 2, res_y, res_xy, gx, gy, *before)
        return norm_call(col, 3, res_yc, res_xyc, gx, gy, *before)

    compute(
        2,
        [n.ax, n.ay, n.mx, n.my],
        norm_rest,
        *[n.res_c, n.res_xc, n.res_y, n.res_xy, n.res_yc, n.res_xyc, n.gx, n.gy, n.norm0],
    )

    send(3, n.cot_x, swap_row, n.cot)
    in_bias_mine = lax.dynamic_slice_in_dim(in_bias, row * units, units, 0)
    compute(3, [n.active, n.slope], pre_call, n.mx, n.my, n.wx, n.wy0, n.wy1, in_bias_mine)

    def grads(beat, names, cuts, *inputs, **keys):
        compute(beat, names, lambda *a: weight_grad(cuts, *a, **keys), *inputs)

    two = [units // 2] * 2
    half_units = [units // 2]
    grads(3, [n.out_own0], half_units, n.active, n.g, vmem=58)
    z = 4
    for i in range(2):
        send(z + i, (n.oy, i), swap_row, (n.oy_sent, i))
    oy = [(n.oy, 0), (n.oy, 1)]
    compute(z, [n.out_own1], lambda a, g: weight_grad(half_units, (a, units // 2), g, vmem=58), n.active, n.g)
    share(z, n.h, gather_col, n.cot_x)
    compute(z, n.x_near, below, n.res, n.res_y)
    compute(z, n.y_near, below, n.res_x, n.res_xy)
    compute(z, n.x_far, below, n.res_c, n.res_yc)
    compute(z, n.y_far, below, n.res_xc, n.res_xyc)
    grads(z + 1, [n.out_oth0, n.out_oth1], two, n.active, n.h, vmem=58)
    compute(z + 2, [n.pre_grad, n.in_bias_sum], pre_grad_call, n.g, n.h, n.ox, *oy, n.slope)
    two = [feats // 2] * 2
    grads(z + 3, [n.in_own0, n.in_own1], two, n.mx, n.pre_grad)
    grads(z + 3, [n.in_oth0, n.in_oth1], two, n.my, n.pre_grad)
    cut = 5 * feats // 8
    for i, (lo, hi) in enumerate(((0, cut), (cut, feats))):
        sent = (n.qy_sent, i)
        compute(2, sent, lambda w, lo=lo, hi=hi: lax.dynamic_index_in_dim(w[lo:hi], other, 1, False), qkv_weight)
        send(z + 2 + i, (n.qy, i), swap_row, sent)
    send(z + 3, n.dy, swap_row, n.dense_sent)
    compute(z + 4, n.qy, below, (n.qy, 0), (n.qy, 1))
    qkv_bias_mine = lax.dynamic_index_in_dim(qkv_bias, row, 0, False)
    compute(
        z + 4,
        [n.query, n.key, n.value],
        packed_call,
        *[n.ax, n.ay, n.qx, n.qy, qkv_bias_mine, n.cos, n.low, n.high],
    )
    compute(
        z + 4,
        n.attended_grad,
        lambda g, h, dx, dy: (dot(g, dx, NT) + dot(h, dy, NT)).astype(BF),
        *[n.g, n.h, n.dx, n.dy],
    )
    compute(
        z + 5,
        [n.packed_grad, n.attended, n.qkv_bias_sum],
        lambda *a: attention(slots, *a),
        *[n.query, n.key, n.value, n.attended_grad, n.cos, n.low, n.high],
    )
    cuts = [2 * HS, 2 * HS]
    grads(z + 6, [n.att_own0, n.att_own1], cuts, n.packed_grad, n.ax, n.attended, n.g)
    grads(z + 6, [n.att_oth0, n.att_oth1], cuts, n.packed_grad, n.ay, n.attended, n.h)

    send(z + 4, n.in_oth0_x, swap_row, n.in_oth0)
    send(z + 5, n.in_oth1_x, swap_row, n.in_oth1)
    send(z + 7, n.att_oth0_x, swap_row, n.att_oth0)
    send(z + 8, n.att_oth1_x, swap_row, n.att_oth1)
    plan.line.enter(
        *(n.out_own0, n.out_own1, n.out_oth0, n.out_oth1, n.in_own0, n.in_own1, n.in_oth0_x),
        *(n.att_own0, n.att_own1, n.att_oth0_x, n.att_oth1_x, n.in_oth1_x, n.small),
    )

    def choose_part(parts):
        return choose(parts[0])(parts[2], parts[1])

    compute(z + 5, n.out_oth0_s, choose_part, (n.out_oth0, n.parts))
    compute(z + 7, n.out_oth1_s, choose_part, (n.out_oth1, n.parts))
    send(z + 6, n.out_oth0_y, swap_row, n.out_oth0_s)
    send(z + 9, n.out_oth1_y, swap_row, n.out_oth1_s)

    for beat, part, name, sums, x, y in (
        (z + 7, 1, (n.ng, n.far), n.sums_far, n.x_far, n.y_far),
        (z + 8, 0, (n.ng, n.near), n.sums_near, n.x_near, n.y_near),
    ):
        compute(
            beat,
            [name, sums],
            lambda *a, part=part: norm_grad_call(col, part, *a),
            *[x, y, n.gx, n.gy, n.packed_grad, n.pre_grad, n.qx, n.qy, n.wx, n.wy0, n.wy1],
        )
    for beat, part, name in ((z + 9, 1, (n.mixed, n.far)), (z + 10, 0, (n.mixed, n.near))):
        compute(
            beat,
            name,
            lambda *a, part=part: mixed_call(col, part, *a),
            *[n.attended, n.active, n.dx, n.dy, n.ox, *oy],
        )

    part_rows = rows // 2

    def near_sum(a, b, c):
        out = a.astype(F32) + b.astype(F32) + c.astype(F32)
        return [out[:, feats:].astype(BF), out[:, :feats]]

    outs = [(feats, BF), (feats, F32)]

    def near_part(i, join=False):
        at = i * part_rows

        def fn(a, b, c, *before):
            keys = dict(whole=rows, skip=at, before=before) if join else {}
            return rowwise(near_sum, part_rows, outs, (a, at), (b, at), c, vmem=58, **keys)

        return fn

    def far_sum(i):
        at, outs = rows + i * part_rows, [(width, BF)]
        return lambda a, b: rowwise(plain_add, part_rows, outs, (a, at), (b, at), vmem=58)[0]

    def scatter(beat, name, last=False):
        far, mine, got = [(name, i) for i in (n.far, n.near, n.core)]
        send(beat, got, swap_core, far, 0)
        got_y = [(name, n.near, i) for i in range(2)]
        for i in range(2):
            far_y = (name, n.far, i)
            compute(beat + i, far_y, far_sum(i), mine, got)
            send(beat + 1 + i, got_y[i], swap_y, far_y)
        if last:
            for i in range(2):
                sent = (name, n.sent, i)
                compute(beat + 2 + i, [sent, (name, n.keep, i)], near_part(i), mine, got, got_y[i], top=i == 1)
                send(beat + 3, (name, n.got, i), swap_row, sent)
            return
        half_sent, half_keep = [(name, part, 0) for part in (n.sent, n.keep)]
        compute(beat + 2, [half_sent, half_keep], near_part(0, True), mine, got, got_y[0])
        last_part = [near_part(1, True), mine, got, got_y[1], half_sent, half_keep]
        compute(beat + 3, [(name, n.sent), (name, n.keep)], *last_part, top=True)
        send(beat + 3, (name, n.got), swap_row, (name, n.sent))

    scatter(z + 8, n.ng)
    compute(
        z + 14,
        n.block_out,
        lambda a0, a1, x0, x1, res, b, c: (
            res.astype(F32) + below(a0, a1) + below(x0, x1).astype(F32) + b + c
        ).astype(BF),
        *[(n.mixed, part, i) for part in (n.keep, n.got) for i in range(2)],
        *[n.res, dense_bias, out_bias],
    )

    def own_norm(res, res_x):
        x, y = res.astype(F32), res_x.astype(F32)
        average = (jnp.sum(x, 1, keepdims=True) + jnp.sum(y, 1, keepdims=True)) / width
        squares = (jnp.sum(x * x, 1, keepdims=True) + jnp.sum(y * y, 1, keepdims=True)) / width
        scale = lax.rsqrt(squares - average * average + EPSILON)
        return (x - average) * scale, scale

    def token_sums(keep, xg, res, res_x):
        normed, scale = own_norm(res, res_x)
        grad = keep + xg.astype(F32)
        return jnp.stack([jnp.sum(grad, 1), jnp.sum(grad * normed, 1)])

    compute(z + 12, n.tok, token_sums, (n.ng, n.keep), (n.ng, n.got), n.res, n.res_x)
    send(z + 12, n.tok_x, swap_row, n.tok, 0)

    def finish_input(keep, xg, res, res_x, cot, tok, tok_x):
        normed, scale = own_norm(res, res_x)
        tok = (tok + tok_x) / width
        grad = keep + xg.astype(F32)
        return cot.astype(F32) + scale * (grad - tok[0][:, None] - normed * tok[1][:, None])

    rest = [n.res, n.res_x, n.cot, n.tok, n.tok_x]
    compute(
        z + 12, n.input_grad, finish_input, (n.ng, n.keep), (n.ng, n.got), *rest
    )

    def small_all(near, far, cot, qkv_bias_sum, in_bias_sum):
        bias_sum = jnp.pad(jnp.sum(cot, 0, dtype=F32), (0, feats))
        parts = [(near + far).reshape(-1), bias_sum, qkv_bias_sum.reshape(-1), in_bias_sum.reshape(-1)]
        return jnp.concatenate(parts)

    def take(parts):
        return jnp.where(parts[0], parts[1], parts[2])

    compute(z + 8, n.small, small_all, n.sums_near, n.sums_far, n.cot, n.qkv_bias_sum, n.in_bias_sum)
    compute(z + 12, n.small_s, take, (n.small, n.parts), top=True)
    send(z + 12, n.small_x, swap_row, n.small_s)

    def by_feature(mine, got):
        mine, got = (v[: 5 * width].reshape(5, width) for v in (mine, got))
        return mine[:, :feats] + got[:, feats:]

    compute(z + 13, n.small0, by_feature, n.small_s, n.small_x)
    send(z + 13, n.small0_c, swap_core, n.small0, 0)
    compute(z + 13, n.small1, jnp.add, n.small0, n.small0_c)
    send(z + 13, n.small1_y, swap_y, n.small1, 0)
    compute(z + 13, n.small2, jnp.add, n.small1, n.small1_y)

    def finish(beat, name, fn, *sources):
        def step(*sources):
            flag = next(v[0] for v in sources if isinstance(v, tuple))
            arrays = [v[1:] if isinstance(v, tuple) else (v,) for v in sources]
            return fn(jnp.stack([row, flag.astype(jnp.int32)]), arrays)

        compute(beat, name, step, *sources)

    def done(*names):
        return [(v, n.parts) for v in names]

    finish(z + 11, n.out_weight_grad, finish_out, *done(n.out_own0, n.out_own1), n.out_oth0_y, n.out_oth1_y)
    att = done(n.att_own0, n.att_own1, n.att_oth0_x, n.att_oth1_x)
    finish(z + 13, n.qkv_weight_grad, finish_qkv, *att)
    finish(z + 13, n.dense_weight_grad, finish_dense, att[1], att[3])
    finish(z + 12, n.in_grad0, finish_in, *done(n.in_own0, n.in_oth0_x))

    def second(meta, arrays):
        return finish_in(meta, arrays[:2], arrays[2][0])

    finish(z + 14, n.in_weight_grad, second, *done(n.in_own1, n.in_oth1_x), n.in_grad0)
    scatter(z + 10, n.mixed, last=True)
    plan.run()
    def in_order(mine, got):
        return jnp.where(row == 0, jnp.concatenate([mine, got]), jnp.concatenate([got, mine]))

    by_feature = env[n.small2]
    by_col, by_col_got = (env[name][5 * width :] for name in (n.small_s, n.small_x))
    qkv_bias_grad = in_order(by_col[: 3 * HS], by_col_got[: 3 * HS]).reshape(2, 3 * HS)
    in_bias_grad = in_order(by_col[3 * HS :], by_col_got[3 * HS :])
    return (
        env[n.block_out],
        env[n.input_grad],
        by_feature[0],
        by_feature[1],
        by_feature[2],
        by_feature[3],
        env[n.qkv_weight_grad],
        qkv_bias_grad,
        env[n.dense_weight_grad],
        by_feature[4],
        env[n.in_weight_grad],
        in_bias_grad,
        env[n.out_weight_grad],
        by_feature[4],
    )


def solution(mesh):
    in_specs = (
        P(("dp", "col"), "row"),
        P("row"),
        P("row"),
        P("row"),
        P("row"),
        P("row", "col", None),
        P("col", None),
        P("col", None, "row"),
        P("row"),
        P("row", "col"),
        P("col"),
        P("col", "row"),
        P("row"),
        P(("dp", "col"), "row"),
    )
    out_specs = (
        P(("dp", "col"), "row"),
        P(("dp", "col"), "row"),
        P("row"),
        P("row"),
        P("row"),
        P("row"),
        P("row", "col", None),
        P("col", None),
        P("col", None, "row"),
        P("row"),
        P("row", "col"),
        P("col"),
        P("col", "row"),
        P("row"),
    )
    return jax.shard_map(
        per_device, mesh=mesh, in_specs=in_specs, out_specs=out_specs, check_vma=False
    )
```
